128 devices in a mesh: lon: 16 (over x_hi, z, core), lat: 8 (over y, x_lo).
Axes of the slice: x: 4 (x_hi: 2, x_lo: 2; x = x_hi * 2 + x_lo), y: 4, z: 4, core: 2. Of those that a mesh axis runs over, the one named last changes fastest.
Arguments:
- heat_anomaly_values: float32 [10, 512, 4096], P(None, 'lat', 'lon'), may hold values from -6 to 6
- saltiness_anomaly: float32 [10, 512, 4096], P(None, 'lat', 'lon'), may hold values from -6 to 6
- zonal_speed: float32 [10, 512, 4096], P(None, 'lat', 'lon'), may hold values from -3 to 3
- meridional_speed: float32 [10, 512, 4096], P(None, 'lat', 'lon'), may hold values from -3 to 3
- marine_site_indicator: int32 [10, 512, 4096], P(None, 'lat', 'lon'), may hold values 0 or 1
- layer_boundary_mixing_rate: float32 [9, 512, 4096], P(None, 'lat', 'lon'), may hold values from 0.05 to 5
- layer_spacing: float32 [10], replicated, may hold values from 0.5 to 2
- planetary_spin_rate: float32 [512], P('lat'), may hold values from 0.4 to 2
- seam_hinge_variety: int32 [1], replicated, may hold values from 0 to 1
- seam_partner_meridian: int32 [4096], P('lon'), may hold values from 0 to 4095, as said below
Outputs:
- temperature_next: float32 [10, 512, 4096], P(None, 'lat', 'lon')
- salinity_next: float32 [10, 512, 4096], P(None, 'lat', 'lon')
- eastward_next: float32 [10, 512, 4096], P(None, 'lat', 'lon')
- northward_next: float32 [10, 512, 4096], P(None, 'lat', 'lon')
The draws below stay inside these ranges and needn't reach their ends.
Inputs may be any that keep to these rules, and one draw needn't show every extreme that they name: seam_partner_meridian[i] = (c * 256 - 1 - i) mod 4096 for one whole number c drawn for the run: each longitude is paired with its mirror about a tile boundary.
All inputs are finite; a program needn't handle non-finite values. No bound on the sum of `marine_site_indicator` on one device may be relied on, other than what follows from the above.
Results may differ from the reference program's by a relative error of at most 0.00002.
Values sent between devices are 32-bit elements; how exact they have to be, the bound alone decides.
No kernel may reach another device: no remote copies, remote signals or barrier semaphores. Data moves between devices by JAX's collectives and lax.ppermute only.
A program may use at most 128 MiB of HBM per device.

```python
import math
import jax
import jax.numpy as jnp
from jax import lax

NI_DEV = 256
VERTICAL_LAYERS = 10
ZONAL_POINTS = 4096
MERIDIONAL_ROWS = 512


def draw_seam_partner_meridian(key, part):
    key = jax.random.fold_in(key, 11)
    tile_count = ZONAL_POINTS // NI_DEV
    anchor = jax.random.randint(key, (), 0, tile_count, dtype=jnp.int32) * NI_DEV - 1
    columns = jnp.arange(ZONAL_POINTS, dtype=jnp.int32)
    return jnp.mod(anchor - columns, ZONAL_POINTS).astype(jnp.int32)


def touch_ends(values, own_key, smallest, high):
    longest = values.shape.index(max(values.shape))
    spots = []
    for shift in (0, 1):
        where = [jax.random.randint(jax.random.fold_in(own_key, axis), (), 0, length) for axis, length in enumerate(values.shape)]
        where[longest] = (where[longest] + shift) % values.shape[longest]
        spots.append(tuple(where))
    return values.at[spots[0]].set(smallest).at[spots[1]].set(high)


def block_scale(own_key, dims, pieces, least, largest):
    gain, own = 1.0, jax.random.fold_in(own_key, 6)
    for dim, shards_of in pieces:
        heights = jnp.exp(jax.random.uniform(jax.random.fold_in(own, dim), (shards_of,), jnp.float32, least / len(pieces), largest / len(pieces)))
        gain = gain * jnp.repeat(heights, dims[dim] // shards_of).reshape([-1 if axis == dim else 1 for axis in range(len(dims))])
    return gain


def noise(rng, dims, spread, bound, cuts=(), kind=jnp.bfloat16):
    array = spread * jax.random.normal(rng, dims, jnp.float32)
    if cuts:
        array = array * block_scale(rng, dims, cuts, -0.22, 0.18)
    return jnp.clip(array, -bound, bound).astype(kind)


def setup_inputs(seed: int = 0) -> dict:
    streams_of = jax.random.split(jax.random.key(seed), 11)
    return {
        "heat_anomaly_values": noise(streams_of[0], (VERTICAL_LAYERS, MERIDIONAL_ROWS, ZONAL_POINTS), 1.0, 6.0, ((1, 8), (2, 16)), jnp.float32),
        "saltiness_anomaly": noise(streams_of[1], (VERTICAL_LAYERS, MERIDIONAL_ROWS, ZONAL_POINTS), 1.0, 6.0, ((1, 8), (2, 16)), jnp.float32),
        "zonal_speed": noise(streams_of[2], (VERTICAL_LAYERS, MERIDIONAL_ROWS, ZONAL_POINTS), 0.5, 3.0, ((1, 8), (2, 16)), jnp.float32),
        "meridional_speed": noise(streams_of[3], (VERTICAL_LAYERS, MERIDIONAL_ROWS, ZONAL_POINTS), 0.5, 3.0, ((1, 8), (2, 16)), jnp.float32),
        "marine_site_indicator": touch_ends((jax.random.randint(streams_of[4], (VERTICAL_LAYERS, MERIDIONAL_ROWS, ZONAL_POINTS), 0, 5) < 4).astype(jnp.int32), jax.random.fold_in(streams_of[4], 1), 0, 1),
        "layer_boundary_mixing_rate": jnp.clip(jnp.exp(math.log(5.0) - 4.6051702 * jax.random.uniform(streams_of[5], (VERTICAL_LAYERS - 1, MERIDIONAL_ROWS, ZONAL_POINTS), jnp.float32) ** block_scale(streams_of[5], (VERTICAL_LAYERS - 1, MERIDIONAL_ROWS, ZONAL_POINTS), ((1, 8), (2, 16)), -0.2, 0.2)), 0.05, 5.0),
        "layer_spacing": jnp.clip(jnp.exp(jax.random.uniform(streams_of[6], (VERTICAL_LAYERS,), jnp.float32, math.log(0.5), math.log(2.0))), 0.5, 2.0),
        "planetary_spin_rate": jnp.clip(0.4 + 1.6 * jax.random.uniform(streams_of[7], (MERIDIONAL_ROWS,), jnp.float32) ** block_scale(streams_of[7], (MERIDIONAL_ROWS,), ((0, 8),), -0.2, 0.2), 0.4, 2.0),
        "seam_hinge_variety": jax.random.randint(streams_of[8], (1,), 0, 2).astype(jnp.int32),
        "seam_partner_meridian": draw_seam_partner_meridian(jax.random.fold_in(streams_of[10], 71), 0),
    }


time_step = 0.2
tracer_mixing = 0.3
momentum_mixing = 0.3
thermal_coeff = 0.2
haline_coeff = 0.8
gravity = 0.1


def extend_ghost_border(field, sign, seam_hinge_variety, seam_partner_meridian):
    row_count = field.shape[1]
    source = lax.dynamic_index_in_dim(field, row_count - 1 - seam_hinge_variety[0], 1, keepdims=False)
    ghost_row = sign * jnp.take(source, seam_partner_meridian, axis=1)
    wrapped = jnp.concatenate([field[..., -1:], field, field[..., :1]], axis=2)
    zero_column = jnp.zeros_like(source[:, :1])
    north_row = jnp.concatenate([zero_column, ghost_row, zero_column], axis=1)[:, None, :]
    south_row = jnp.zeros_like(north_row)
    return jnp.concatenate([south_row, wrapped, north_row], axis=1)


def neighbours(padded):
    return (padded[..., 1:-1, 1:-1], padded[..., 1:-1, 2:], padded[..., 1:-1, :-2],
            padded[..., 2:, 1:-1], padded[..., :-2, 1:-1])


def wet_faces(padded_wet):
    wet_here, wet_e, wet_w, wet_n, wet_s = neighbours(padded_wet)
    return wet_here, wet_here * wet_e, wet_here * wet_w, wet_here * wet_n, wet_here * wet_s


def tendency(scalars_plus_ghost_rim, padded_east, padded_north, face_wet):
    wet_here, wet_east, wet_west, wet_north, wet_south = face_wet
    center, value_east, value_west, value_north, value_south = neighbours(scalars_plus_ghost_rim)
    flow_here, flow_east, flow_west, unused_north, unused_south = neighbours(padded_east)
    turn_here, unused_east, unused_west, turn_north, turn_south = neighbours(padded_north)
    face_east = 0.5 * (flow_here + flow_east)
    face_west = 0.5 * (flow_west + flow_here)
    face_north = 0.5 * (turn_here + turn_north)
    face_south = 0.5 * (turn_south + turn_here)
    flux_east = wet_east * (jnp.maximum(face_east, 0.0) * center + jnp.minimum(face_east, 0.0) * value_east
                            - tracer_mixing * (value_east - center))
    flux_west = wet_west * (jnp.maximum(face_west, 0.0) * value_west + jnp.minimum(face_west, 0.0) * center
                            - tracer_mixing * (center - value_west))
    flux_north = wet_north * (jnp.maximum(face_north, 0.0) * center + jnp.minimum(face_north, 0.0) * value_north
                              - tracer_mixing * (value_north - center))
    flux_south = wet_south * (jnp.maximum(face_south, 0.0) * value_south + jnp.minimum(face_south, 0.0) * center
                              - tracer_mixing * (center - value_south))
    return center - time_step * wet_here * (flux_east - flux_west + flux_north - flux_south)


def laplace(padded, face_wet):
    wet_here, wet_east, wet_west, wet_north, wet_south = face_wet
    center, value_east, value_west, value_north, value_south = neighbours(padded)
    return (wet_east * (value_east - center) + wet_west * (value_west - center)
            + wet_north * (value_north - center) + wet_south * (value_south - center))


def hydrostatic(padded_density, layer_spacing):
    layer_weight = padded_density * layer_spacing[:, None, None]
    above = jnp.cumsum(layer_weight, axis=0) - layer_weight
    return gravity * (above + 0.5 * layer_weight)


def momentum(padded_east, padded_north, pressure, coriolis_rows, face_wet):
    wet_here, wet_east, wet_west, wet_north, wet_south = face_wet
    press_here, press_east, press_west, press_north, press_south = neighbours(pressure)
    grad_east = 0.5 * (wet_east * (press_east - press_here) + wet_west * (press_here - press_west))
    grad_north = 0.5 * (wet_north * (press_north - press_here) + wet_south * (press_here - press_south))
    flow_here = padded_east[:, 1:-1, 1:-1]
    turn_here = padded_north[:, 1:-1, 1:-1]
    new_east = flow_here + time_step * wet_here * (coriolis_rows * turn_here - grad_east
                                                   + momentum_mixing * laplace(padded_east, face_wet))
    new_north = turn_here + time_step * wet_here * (-coriolis_rows * flow_here - grad_north
                                                    + momentum_mixing * laplace(padded_north, face_wet))
    return jnp.stack([new_east, new_north])


def factor(marine_sites, layer_boundary_mixing_rate, layer_spacing):
    kappa = layer_boundary_mixing_rate * marine_sites[:-1] * marine_sites[1:]
    level_count = marine_sites.shape[0]
    bands = []
    previous = None
    for layer in range(level_count):
        height = layer_spacing[layer]
        if layer > 0:
            lower_band = -time_step * kappa[layer - 1] / height
        else:
            lower_band = jnp.zeros_like(marine_sites[0])
        if layer < level_count - 1:
            upper_band = -time_step * kappa[layer] / height
        else:
            upper_band = jnp.zeros_like(marine_sites[0])
        divisor = 1.0 - lower_band - upper_band
        if previous is not None:
            divisor = divisor - lower_band * previous
        ratio_band = upper_band / divisor
        bands.append((lower_band, divisor, ratio_band))
        previous = ratio_band
    return bands


def solve_columns(bands, right_side):
    level_count = len(bands)
    forward = []
    previous = None
    for layer in range(level_count):
        lower_band, divisor, ratio_band = bands[layer]
        current = right_side[:, layer]
        if previous is not None:
            current = current - lower_band * previous
        previous = current / divisor
        forward.append(previous)
    result = [None] * level_count
    after = forward[-1]
    result[-1] = after
    for layer in reversed(range(level_count - 1)):
        after = forward[layer] - bands[layer][2] * after
        result[layer] = after
    return jnp.stack(result, axis=1)


def reference(heat_anomaly_values, saltiness_anomaly, zonal_speed, meridional_speed, marine_site_indicator, layer_boundary_mixing_rate, layer_spacing, planetary_spin_rate,
              seam_hinge_variety, seam_partner_meridian):
    marine_sites = marine_site_indicator.astype(jnp.float32)
    face_wet = wet_faces(extend_ghost_border(marine_sites, 1.0, seam_hinge_variety, seam_partner_meridian))
    scalars_plus_ghost_rim = jnp.stack([extend_ghost_border(heat_anomaly_values, 1.0, seam_hinge_variety, seam_partner_meridian),
                                extend_ghost_border(saltiness_anomaly, 1.0, seam_hinge_variety, seam_partner_meridian)])
    padded_east = extend_ghost_border(zonal_speed, -1.0, seam_hinge_variety, seam_partner_meridian)
    padded_north = extend_ghost_border(meridional_speed, -1.0, seam_hinge_variety, seam_partner_meridian)
    tracer_step = tendency(scalars_plus_ghost_rim, padded_east, padded_north, face_wet)
    bands = factor(marine_sites, layer_boundary_mixing_rate, layer_spacing)
    new_tracers = solve_columns(bands, tracer_step)
    density = -thermal_coeff * new_tracers[0] + haline_coeff * new_tracers[1]
    pressure = hydrostatic(extend_ghost_border(density, 1.0, seam_hinge_variety, seam_partner_meridian), layer_spacing)
    flow_step = momentum(padded_east, padded_north, pressure, planetary_spin_rate[None, :, None], face_wet)
    new_flows = solve_columns(bands, flow_step)
    return new_tracers[0], new_tracers[1], new_flows[0], new_flows[1]
```

```python
import functools

import jax
import jax.numpy as jnp
from jax import lax
from jax.experimental import pallas as pl
from jax.experimental.pallas import tpu as pltpu
from jax.sharding import PartitionSpec as P

LEVELS = 10
ROWS = 64
COLS = 256
TILE = 8
LANES = 128
HEAT, SALT, EAST, NORTH, WET, PART, MIX = 0, 10, 20, 30, 40, 50, 60
PAYLOAD = 72
SOUTH_LANE, NORTH_LANE = 64, 65
F_ROW = 40
EAST_SIDE = 48
GRAIN = 0.06


def iota(shape, dim):
    return lax.broadcasted_iota(jnp.int32, shape, dim)


def weights(wet_a, wet_b, speed_a, speed_b):
    both = wet_a * wet_b
    speed = 0.1 * (speed_a + speed_b)
    return both * (jnp.maximum(speed, 0.0) + GRAIN), both * (jnp.minimum(speed, 0.0) - GRAIN)


def east_of(x):
    return pltpu.roll(x, x.shape[1] - 1, 1)


def west_of(x):
    return pltpu.roll(x, 1, 1)


def north_of(x, block_above, sub):
    return pltpu.roll(jnp.where(sub == 0, block_above, x), TILE - 1, 0)


def south_of(x, block_below, sub):
    return pltpu.roll(jnp.where(sub == TILE - 1, block_below, x), 1, 0)


def mix_down(heat, salt):
    return 0.8 * salt - 0.2 * heat


def pack_rows(hinge_ref, *refs):
    bottom, top, (a_ref, b_ref) = refs[:6], refs[6:12], refs[12:]
    lat = lax.axis_index("lat")
    at_top = lat == lax.axis_size("lat") - 1
    even = lat % 2 == 0
    hinged = jnp.logical_and(at_top, hinge_ref[0] == 1)
    inner = (iota((TILE, COLS), 1) < COLS - 1).astype(jnp.float32)
    sub = iota((TILE, COLS), 0)
    for level in range(LEVELS):
        sides = []
        for heat_ref, salt_ref, east_ref, north_ref, wet_ref, mix_ref in (bottom, top):
            heat, salt = heat_ref[level], salt_ref[level]
            east, north = east_ref[level], north_ref[level]
            wet = wet_ref[level].astype(jnp.float32)
            mixed = mix_down(heat, salt)
            here, there = weights(wet * inner, east_of(wet), east, east_of(east))
            flux_e = here * mixed + there * east_of(mixed)
            above = lambda x: pltpu.roll(x, TILE - 1, 0)
            here, there = weights(wet, above(wet), north, above(north))
            flux_n = here * mixed + there * above(mixed)
            part = mixed - (flux_e - west_of(flux_e))
            sides.append((heat, salt, east, north, wet, part, mix_ref[min(level, LEVELS - 2)], flux_n))
        *low, flux_n = sides[0]
        low[5] = low[5] - flux_n
        low = [x[:1] for x in low]
        *high, flux_n = sides[1]
        flux_s = pltpu.roll(flux_n, 1, 0)
        high[5] = high[5] + flux_s - jnp.where(sub == TILE - 1, 0.0, flux_n)
        high = [jnp.where(hinged, x[TILE - 2 : TILE - 1], x[TILE - 1 :]) for x in high]
        for start, one, other in zip((HEAT, SALT, EAST, NORTH, WET, PART, MIX), low, high):
            if start == MIX and level == LEVELS - 1:
                continue
            a_ref[start + level : start + level + 1] = jnp.where(even, other, one)
            b_ref[start + level : start + level + 1] = jnp.where(even, one, other)
    for ref in (a_ref, b_ref):
        ref[MIX + LEVELS - 1 :] = jnp.zeros((PAYLOAD - MIX - LEVELS + 1, COLS), jnp.float32)

    @pl.when(at_top)
    def _():
        back = LANES - 1 - iota((TILE, LANES), 1)
        for row in range(0, PAYLOAD, TILE):
            place = row + iota((TILE, LANES), 0)
            sign = jnp.where(jnp.logical_and(place >= EAST, place < WET), -1.0, 1.0)
            left = b_ref[row : row + TILE, :LANES]
            right = b_ref[row : row + TILE, LANES:]
            flip = lambda x: sign * jnp.take_along_axis(x, back, axis=1, mode="promise_in_bounds")
            b_ref[row : row + TILE, :LANES] = flip(right)
            b_ref[row : row + TILE, LANES:] = flip(left)


def from_lat(a_ref, b_ref):
    even = lax.axis_index("lat") % 2 == 0
    a, b = a_ref[...], b_ref[...]
    return jnp.where(even, b, a), jnp.where(even, a, b)


def load(pairs, sems):
    copies = [pltpu.make_async_copy(src, dst, sems.at[i]) for i, (src, dst) in enumerate(pairs)]
    for copy in copies:
        copy.start()
    return copies


def advect(
    hinge_ref, heat_ref, salt_ref, east_ref, north_ref, wet_ref, mix_ref, a_ref, b_ref,
    heat_out, salt_out, rhs_out, c_out, d_out,
    heat_x, salt_x, east_x, north_x, wet_x, mix_x, heat_f, salt_f, rim, ghost, sems,
):
    inside = pl.ds(TILE, ROWS)
    copies = load(
        [
            (heat_ref, heat_x.at[:, inside]),
            (salt_ref, salt_x.at[:, inside]),
            (east_ref, east_x),
            (north_ref, north_x.at[:, inside]),
            (wet_ref, wet_x.at[:, inside]),
            (mix_ref, mix_x),
        ],
        sems,
    )
    lat = lax.axis_index("lat")
    at_top = lat == lax.axis_size("lat") - 1
    open_north = jnp.where(jnp.logical_and(at_top, hinge_ref[0] == 1), 0.0, 1.0)
    ghost[0], ghost[1] = from_lat(a_ref, b_ref)
    inner = (iota((TILE, COLS), 1) < COLS - 1).astype(jnp.float32)
    sub = iota((TILE, COLS), 0)
    lane = iota((TILE, LANES), 1)
    south_row, north_row = TILE - 1, TILE + ROWS
    for level in range(LEVELS):
        for ref, start in ((heat_x, HEAT), (salt_x, SALT), (north_x, NORTH), (wet_x, WET)):
            for side, row in ((0, south_row), (1, north_row)):
                ref[level, row : row + 1] = ghost[side, start + level : start + level + 1].astype(ref.dtype)
    for copy in copies:
        copy.wait()

    def north_faces(level, block):
        rows = pl.ds(pl.multiple_of(block * TILE, TILE), TILE)
        above = pl.ds(pl.multiple_of(block * TILE + TILE, TILE), TILE)
        pick = lambda ref: (ref[level, rows], north_of(ref[level, rows], ref[level, above], sub))
        heat, heat_n = pick(heat_x)
        salt, salt_n = pick(salt_x)
        north, north_n = pick(north_x)
        wet, wet_n = (x.astype(jnp.float32) for x in pick(wet_x))
        here, there = weights(wet, wet_n, north, north_n)
        return heat, salt, wet, here * heat + there * heat_n, here * salt + there * salt_n

    for level in range(LEVELS):
        _, _, _, heat_n, salt_n = north_faces(level, 0)
        heat_f[level], salt_f[level] = heat_n, salt_n
        flux = mix_down(heat_n, salt_n)[TILE - 1 :]
        rhs_out[16 + level : 17 + level] = ghost[0, PART + level : PART + level + 1] - flux

    def step(block, _):
        rows = pl.ds(pl.multiple_of(block * TILE, TILE), TILE)
        west_rim = jnp.zeros((TILE, LANES), jnp.float32)
        east_rim = west_rim
        for level in range(LEVELS):
            heat, salt, wet, heat_n, salt_n = north_faces(level, block + 1)
            east = east_x[level, rows]
            heat_s = south_of(heat_n, heat_f[level], sub)
            salt_s = south_of(salt_n, salt_f[level], sub)
            heat_f[level], salt_f[level] = heat_n, salt_n
            here, there = weights(wet * inner, east_of(wet), east, east_of(east))
            heat_e = here * heat + there * east_of(heat)
            salt_e = here * salt + there * east_of(salt)
            new_heat = heat - ((heat_e - west_of(heat_e)) + (heat_n - heat_s))
            new_salt = salt - ((salt_e - west_of(salt_e)) + (salt_n - salt_s))
            heat_out[level, rows] = new_heat
            salt_out[level, rows] = new_salt
            fields = [
                (HEAT, heat),
                (SALT, salt),
                (EAST, east),
                (NORTH, north_x[level, pl.ds(pl.multiple_of(block * TILE + TILE, TILE), TILE)]),
                (WET, wet),
                (PART, mix_down(new_heat, new_salt)),
            ]
            if level < LEVELS - 1:
                fields.append((MIX, mix_x[level, rows]))
            for start, x in fields:
                place = start + level
                west_rim = jnp.where(lane == place, pltpu.roll(x[:, :LANES], place, 1), west_rim)
                east_rim = jnp.where(lane == place, pltpu.roll(x[:, LANES:], place + 1, 1), east_rim)
        rim[0, rows] = west_rim
        rim[1, rows] = east_rim
        return 0

    lax.fori_loop(0, ROWS // TILE, step, 0)
    for level in range(LEVELS):
        flux = mix_down(heat_f[level], salt_f[level])[TILE - 1 :]
        rhs_out[level : level + 1] = ghost[1, PART + level : PART + level + 1] + open_north * flux
    sides = []
    wide = iota((PAYLOAD, LANES), 1)
    for side, column in ((0, 0), (1, COLS - 1)):
        turned = jnp.transpose(rim[side])[:PAYLOAD]
        turned = jnp.where(wide < ROWS, turned, 0.0)
        for place, which in ((SOUTH_LANE, 0), (NORTH_LANE, 1)):
            turned = jnp.where(wide == place, ghost[which, :, column : column + 1], turned)
        sides.append(turned)
    even = lax.axis_index("lon") % 2 == 0
    c_out[...] = jnp.where(even, sides[1], sides[0])
    d_out[...] = jnp.where(even, sides[0], sides[1])


def factor(thick, mix, wet):
    inverse, weight, ratio = [], [], []
    for level in range(LEVELS):
        diagonal = thick[level]
        if level < LEVELS - 1:
            weight.append((0.2 * mix[level]) * (wet[level] * wet[level + 1]))
            diagonal = diagonal + weight[level]
        if level > 0:
            diagonal = diagonal + weight[level - 1] * (1.0 - ratio[level - 1])
        inverse.append(1.0 / diagonal)
        if level < LEVELS - 1:
            ratio.append(weight[level] * inverse[level])
    return inverse, weight, ratio


def solve(thick, inverse, weight, ratio, right):
    x = []
    for level in range(LEVELS):
        now = thick[level] * right[level]
        if level > 0:
            now = now + weight[level - 1] * x[level - 1]
        x.append(now * inverse[level])
    for level in reversed(range(LEVELS - 1)):
        x[level] = x[level] + ratio[level] * x[level + 1]
    return x


def pressures(thick, density):
    above, out = None, []
    for level in range(LEVELS):
        layer = (0.1 * thick[level]) * density[level]
        out.append(0.5 * layer if above is None else above + 0.5 * layer)
        above = layer if above is None else above + layer
    return out


def finish(
    thick_ref, spin_ref, heat_ref, salt_ref, east_ref, north_ref, wet_ref, mix_ref,
    a_ref, b_ref, rhs_ref, c_own_ref, d_own_ref, c_ref, d_ref,
    heat_out, salt_out, east_out, north_out,
    east_x, north_x, wet_x, mix_x, press_x, inv_x, weight_x, ghost, rims,
    rim_rhs, rim_mix, rim_wet, rim_press, rim_rows, fixes, east_f, north_f, sems,
):
    inside = pl.ds(TILE, ROWS)
    copies = load(
        [
            (east_ref, east_x.at[:, inside]),
            (north_ref, north_x.at[:, inside]),
            (wet_ref, wet_x.at[:, inside]),
            (mix_ref, mix_x),
        ],
        sems,
    )
    thick = [thick_ref[level] for level in range(LEVELS)]
    ghost[0], ghost[1] = from_lat(a_ref, b_ref)
    even = lax.axis_index("lon") % 2 == 0
    rims[0] = jnp.where(even, d_own_ref[...], c_own_ref[...])
    rims[1] = jnp.where(even, d_ref[...], c_ref[...])
    rims[2] = jnp.where(even, c_own_ref[...], d_own_ref[...])
    rims[3] = jnp.where(even, c_ref[...], d_ref[...])
    south_row, north_row = TILE - 1, TILE + ROWS
    for level in range(LEVELS):
        for ref, start in ((east_x, EAST), (north_x, NORTH), (wet_x, WET)):
            for side, row in ((0, south_row), (1, north_row)):
                ref[level, row : row + 1] = ghost[side, start + level : start + level + 1].astype(ref.dtype)

    span = lambda which, start: rims[which, start : start + LEVELS]
    lane = iota((LEVELS, LANES), 1)
    mixed_flux = []
    for side, (left, right) in enumerate(((1, 0), (2, 3))):
        here, there = weights(span(left, WET), span(right, WET), span(left, EAST), span(right, EAST))
        heat_e = here * span(left, HEAT) + there * span(right, HEAT)
        salt_e = here * span(left, SALT) + there * span(right, SALT)
        own = 1.0 if side == 0 else -1.0
        base = side * EAST_SIDE
        fixes[base : base + LEVELS] = own * heat_e
        fixes[base + LEVELS : base + 2 * LEVELS] = own * salt_e
        mixed_flux.append(own * mix_down(heat_e, salt_e))
    rim_rows[0:LEVELS] = span(0, PART) + mixed_flux[0]
    rim_rows[16 : 16 + LEVELS] = span(1, PART) - mixed_flux[0]
    rim_rows[32 : 32 + LEVELS] = span(2, PART) + mixed_flux[1]
    rim_rows[48 : 48 + LEVELS] = span(3, PART) - mixed_flux[1]
    for side, (start, end) in ((1, (0, NORTH_LANE)), (0, (16, SOUTH_LANE))):
        low = rhs_ref[start : start + LEVELS, :LANES]
        high = rhs_ref[start : start + LEVELS, LANES:]
        low = low + jnp.where(lane == 0, mixed_flux[0][:, end : end + 1], 0.0)
        high = high + jnp.where(lane == LANES - 1, mixed_flux[1][:, end : end + 1], 0.0)
        base = 64 + 32 * (1 - side)
        rim_rows[base : base + LEVELS] = low
        rim_rows[base + 16 : base + 16 + LEVELS] = high
    for level in range(LEVELS):
        for slot in range(TILE):
            rim_rhs[level, slot : slot + 1] = rim_rows[16 * slot + level : 16 * slot + level + 1]
            for ref, start in ((rim_mix, MIX), (rim_wet, WET)):
                row = slice(start + level, start + level + 1)
                if slot < 4:
                    value = rims[slot, row]
                else:
                    half = (slot % 2) * LANES
                    value = ghost[1 - (slot - 4) // 2, row, half : half + LANES]
                ref[level, slot : slot + 1] = value
    listed = lambda ref: [ref[level] for level in range(LEVELS)]
    bands = factor(thick, listed(rim_mix), listed(rim_wet))
    rim_density = solve(thick, *bands, listed(rim_rhs))
    for level, value in enumerate(pressures(thick, rim_density)):
        rim_press[level] = value
        for slot in range(4):
            rim_rows[16 * slot + level : 16 * slot + level + 1] = rim_press[level, slot : slot + 1]
        press_x[level, north_row : north_row + 1, :LANES] = rim_press[level, 4:5]
        press_x[level, north_row : north_row + 1, LANES:] = rim_press[level, 5:6]
        press_x[level, south_row : south_row + 1, :LANES] = rim_press[level, 6:7]
        press_x[level, south_row : south_row + 1, LANES:] = rim_press[level, 7:8]
    for side, (left, right) in enumerate(((1, 0), (2, 3))):
        both = span(left, WET) * span(right, WET)
        own = -1.0 if side == 0 else 1.0
        slope = 0.1 * both * (
            rim_rows[16 * right : 16 * right + LEVELS] - rim_rows[16 * left : 16 * left + LEVELS]
        )
        base = side * EAST_SIDE + 2 * LEVELS
        fixes[base : base + LEVELS] = own * GRAIN * both * (span(right, EAST) - span(left, EAST)) - slope
        fixes[base + LEVELS : base + 2 * LEVELS] = own * GRAIN * both * (span(right, NORTH) - span(left, NORTH))
    fixes[F_ROW : F_ROW + 1, :ROWS] = 0.2 * spin_ref[...]
    fixes[...] = jnp.transpose(fixes[...])

    for copy in copies:
        copy.wait()
    sub = iota((TILE, COLS), 0)
    lanes = iota((TILE, LANES), 1)
    inner = (iota((TILE, COLS), 1) < COLS - 1).astype(jnp.float32)

    def fix(corner, which, level):
        place = which * LEVELS + level
        west = jnp.where(lanes == 0, pltpu.roll(corner, (LANES - place) % LANES, 1), 0.0)
        place = place + EAST_SIDE
        east = jnp.where(lanes == LANES - 1, pltpu.roll(corner, LANES - 1 - place, 1), 0.0)
        return jnp.concatenate([west, east], axis=1)

    def tracers(block, _):
        rows = pl.ds(pl.multiple_of(block * TILE, TILE), TILE)
        rows_x = pl.ds(pl.multiple_of(block * TILE + TILE, TILE), TILE)
        corner = fixes[rows]
        wet = [wet_x[level, rows_x].astype(jnp.float32) for level in range(LEVELS)]
        mix = [mix_x[level, rows] for level in range(LEVELS - 1)]
        inverse, weight, ratio = factor(thick, mix, wet)
        for level in range(LEVELS):
            inv_x[level, rows] = inverse[level]
            if level < LEVELS - 1:
                weight_x[level, rows] = weight[level]
        heat = [heat_ref[level, rows] + fix(corner, 0, level) for level in range(LEVELS)]
        salt = [salt_ref[level, rows] + fix(corner, 1, level) for level in range(LEVELS)]
        heat = solve(thick, inverse, weight, ratio, heat)
        salt = solve(thick, inverse, weight, ratio, salt)
        density = [mix_down(h, s) for h, s in zip(heat, salt)]
        for level, value in enumerate(pressures(thick, density)):
            heat_out[level, rows] = heat[level]
            salt_out[level, rows] = salt[level]
            press_x[level, rows_x] = value
        return 0

    lax.fori_loop(0, ROWS // TILE, tracers, 0)

    def north_faces(level, block):
        rows = pl.ds(pl.multiple_of(block * TILE, TILE), TILE)
        above = pl.ds(pl.multiple_of(block * TILE + TILE, TILE), TILE)
        pick = lambda ref: (ref[level, rows], north_of(ref[level, rows], ref[level, above], sub))
        east, east_n = pick(east_x)
        north, north_n = pick(north_x)
        press, press_n = pick(press_x)
        wet, wet_n = (x.astype(jnp.float32) for x in pick(wet_x))
        both = wet * wet_n
        spread = GRAIN * both
        slope = (0.1 * both) * (press_n - press)
        return east, north, press, wet, spread * (east_n - east), spread * (north_n - north), slope

    for level in range(LEVELS):
        *_, lap_east, lap_north, slope = north_faces(level, 0)
        east_f[level] = lap_east
        north_f[level] = lap_north + slope

    def flow(block, _):
        rows = pl.ds(pl.multiple_of(block * TILE, TILE), TILE)
        corner = fixes[rows]
        spin = jnp.broadcast_to(corner[:, F_ROW : F_ROW + 1], (TILE, COLS))
        new_east, new_north = [], []
        for level in range(LEVELS):
            east, north, press, wet, lap_east, lap_north, slope = north_faces(level, block + 1)
            from_south = south_of(lap_east, east_f[level], sub)
            push_south = south_of(lap_north + slope, north_f[level], sub)
            east_f[level] = lap_east
            north_f[level] = lap_north + slope
            both = wet * inner * east_of(wet)
            spread = GRAIN * both
            lap_east_e = spread * (east_of(east) - east)
            lap_north_e = spread * (east_of(north) - north)
            slope_e = (0.1 * both) * (east_of(press) - press)
            turn = wet * spin
            new_east.append(
                east + turn * north + (lap_east_e - slope_e) - west_of(lap_east_e + slope_e)
                + (lap_east - from_south) + fix(corner, 2, level)
            )
            new_north.append(
                north - turn * east + (lap_north_e - west_of(lap_north_e))
                + (lap_north - slope) - push_south + fix(corner, 3, level)
            )
        inverse = [inv_x[level, rows] for level in range(LEVELS)]
        weight = [weight_x[level, rows] for level in range(LEVELS - 1)]
        ratio = [weight[level] * inverse[level] for level in range(LEVELS - 1)]
        for out, right in ((east_out, new_east), (north_out, new_north)):
            for level, value in enumerate(solve(thick, inverse, weight, ratio, right)):
                out[level, rows] = value
        return 0

    lax.fori_loop(0, ROWS // TILE, flow, 0)


def swap_in_pairs(x, axis, first):
    count = lax.axis_size(axis)
    return lax.ppermute(x, axis, [(i, (((i - first) ^ 1) + first) % count) for i in range(count)])


def swap_with_fold(x, anchor):
    lon, lat = lax.axis_size("lon"), lax.axis_size("lat")
    pairs = []
    for i in range(lon):
        for j in range(1, lat - 1):
            pairs.append((i * lat + j, i * lat + ((j - 1) ^ 1) + 1))
        pairs.append((i * lat + lat - 1, (anchor - 1 - i) % lon * lat + lat - 1))
    return lax.ppermute(x, ("lon", "lat"), pairs)


def on_device(heat, salt, east, north, marine, mixing, spacing, spin, hinge, partner):
    f32, i32 = jnp.float32, jnp.int32
    lon = lax.axis_size("lon")
    anchor = (partner[0] + 1 + COLS * lax.axis_index("lon")) // COLS % lon
    smem = pl.BlockSpec(memory_space=pltpu.SMEM)
    vmem = pl.BlockSpec(memory_space=pltpu.VMEM)
    anywhere = pl.BlockSpec(memory_space=pl.ANY)
    shape = jax.ShapeDtypeStruct
    cells = (heat, salt, east, north, marine, mixing)
    edge = [
        pl.BlockSpec((x.shape[0], TILE, COLS), lambda i, at=at: (0, at, 0))
        for at in (0, ROWS // TILE - 1)
        for x in cells
    ]
    a_sent, b_sent = pl.pallas_call(
        pack_rows,
        grid=(1,),
        in_specs=[smem] + edge,
        out_specs=[pl.BlockSpec((PAYLOAD, COLS), lambda i: (0, 0))] * 2,
        out_shape=[shape((PAYLOAD, COLS), f32)] * 2,
        name="pack_rows",
    )(hinge, *cells, *cells)
    a_got = swap_in_pairs(a_sent, "lat", 0)
    b_got = lax.switch(anchor, [functools.partial(swap_with_fold, anchor=k) for k in range(lon)], b_sent)
    wide = (LEVELS, ROWS + 2 * TILE, COLS)
    plain = (LEVELS, ROWS, COLS)
    heat_step, salt_step, rhs, c_sent, d_sent = pl.pallas_call(
        advect,
        in_specs=[smem] + [anywhere] * 6 + [vmem] * 2,
        out_specs=[vmem] * 5,
        out_shape=[shape(plain, f32)] * 2 + [shape((32, COLS), f32)] + [shape((PAYLOAD, LANES), f32)] * 2,
        scratch_shapes=[
            pltpu.VMEM(wide, f32),
            pltpu.VMEM(wide, f32),
            pltpu.VMEM(plain, f32),
            pltpu.VMEM(wide, f32),
            pltpu.VMEM(wide, i32),
            pltpu.VMEM((LEVELS - 1, ROWS, COLS), f32),
            pltpu.VMEM((LEVELS, TILE, COLS), f32),
            pltpu.VMEM((LEVELS, TILE, COLS), f32),
            pltpu.VMEM((2, LANES, LANES), f32),
            pltpu.VMEM((2, PAYLOAD, COLS), f32),
            pltpu.SemaphoreType.DMA((6,)),
        ],
        compiler_params=pltpu.CompilerParams(vmem_limit_bytes=40 * 2**20),
        name="advect",
    )(hinge, *cells, a_got, b_got)
    c_got = swap_in_pairs(c_sent, "lon", 0)
    d_got = swap_in_pairs(d_sent, "lon", 1)
    return pl.pallas_call(
        finish,
        in_specs=[smem] + [vmem] * 3 + [anywhere] * 4 + [vmem] * 7,
        out_specs=[vmem] * 4,
        out_shape=[shape(plain, f32)] * 4,
        scratch_shapes=[
            pltpu.VMEM(wide, f32),
            pltpu.VMEM(wide, f32),
            pltpu.VMEM(wide, i32),
            pltpu.VMEM((LEVELS - 1, ROWS, COLS), f32),
            pltpu.VMEM(wide, f32),
            pltpu.VMEM(plain, f32),
            pltpu.VMEM(plain, f32),
            pltpu.VMEM((2, PAYLOAD, COLS), f32),
            pltpu.VMEM((4, PAYLOAD, LANES), f32),
            pltpu.VMEM((LEVELS, TILE, LANES), f32),
            pltpu.VMEM((LEVELS, TILE, LANES), f32),
            pltpu.VMEM((LEVELS, TILE, LANES), f32),
            pltpu.VMEM((LEVELS, TILE, LANES), f32),
            pltpu.VMEM((LANES, LANES), f32),
            pltpu.VMEM((LANES, LANES), f32),
            pltpu.VMEM((LEVELS, TILE, COLS), f32),
            pltpu.VMEM((LEVELS, TILE, COLS), f32),
            pltpu.SemaphoreType.DMA((4,)),
        ],
        compiler_params=pltpu.CompilerParams(vmem_limit_bytes=48 * 2**20),
        name="finish",
    )(
        spacing, spin.reshape(1, -1), heat_step, salt_step, east, north, marine, mixing,
        a_got, b_got, rhs, c_sent, d_sent, c_got, d_got,
    )


def solution(mesh):
    cells = P(None, "lat", "lon")
    return jax.shard_map(
        on_device,
        mesh=mesh,
        in_specs=(cells,) * 6 + (P(), P("lat"), P(), P("lon")),
        out_specs=(cells,) * 4,
        check_vma=False,
    )
```

```python
import functools

import jax
import jax.numpy as jnp
from jax import lax
from jax.experimental import pallas as pl
from jax.experimental.pallas import tpu as pltpu
from jax.sharding import PartitionSpec as P

LEVELS = 10
ROWS = 64
COLS = 256
TILE = 8
BLOCKS = ROWS // TILE
LANES = 128
GROUP = 16
HEAT, SALT, EAST, NORTH, WET, PART, MIX = 0, 10, 20, 30, 40, 50, 60
PAYLOAD = 72
SOUTH_LANE, NORTH_LANE = 64, 65
GRAIN = 0.06
DRY = 1.0e30


def iota(shape, dim):
    return lax.broadcasted_iota(jnp.int32, shape, dim)


def weights(both, speeds):
    speed = 0.1 * speeds
    return both * (jnp.maximum(speed, 0.0) + GRAIN), both * (jnp.minimum(speed, 0.0) - GRAIN)


def east_of(x):
    return pltpu.roll(x, x.shape[1] - 1, 1)


def west_of(x):
    return pltpu.roll(x, 1, 1)


def north_of(x, block_above, sub):
    return pltpu.roll(jnp.where(sub == 0, block_above, x), TILE - 1, 0)


def south_of(x, block_below, sub):
    return pltpu.roll(jnp.where(sub == TILE - 1, block_below, x), 1, 0)


def mix_down(heat, salt):
    return 0.8 * salt - 0.2 * heat


def tile_rows(block):
    return pl.ds(pl.multiple_of(block * TILE, TILE), TILE)


def pack_rows(hinge_ref, *refs):
    bottom, top, (a_ref, b_ref, own_ref) = refs[:6], refs[6:12], refs[12:]
    lat = lax.axis_index("lat")
    at_top = lat == lax.axis_size("lat") - 1
    even = lat % 2 == 0
    hinged = jnp.logical_and(at_top, hinge_ref[0] == 1)
    inner = (iota((TILE, COLS), 1) < COLS - 1).astype(jnp.float32)
    sub = iota((TILE, COLS), 0)
    for level in range(LEVELS):
        sides = []
        for heat_ref, salt_ref, east_ref, north_ref, wet_ref, mix_ref in (bottom, top):
            heat, salt = heat_ref[level], salt_ref[level]
            east, north = east_ref[level], north_ref[level]
            wet = wet_ref[level].astype(jnp.float32)
            mixed = mix_down(heat, salt)
            here, there = weights(wet * inner * east_of(wet), east + east_of(east))
            flux_e = here * mixed + there * east_of(mixed)
            above = lambda x: pltpu.roll(x, TILE - 1, 0)
            here, there = weights(wet * above(wet), north + above(north))
            flux_n = here * mixed + there * above(mixed)
            part = mixed - (flux_e - west_of(flux_e))
            sides.append((heat, salt, east, north, wet, part, mix_ref[min(level, LEVELS - 2)], flux_n))
        *low, flux_n = sides[0]
        low[5] = low[5] - flux_n
        low = [x[:1] for x in low]
        *high, flux_n = sides[1]
        flux_s = pltpu.roll(flux_n, 1, 0)
        high[5] = high[5] + flux_s - jnp.where(sub == TILE - 1, 0.0, flux_n)
        last = [x[TILE - 1 :] for x in high]
        high = [jnp.where(hinged, x[TILE - 2 : TILE - 1], end) for x, end in zip(high, last)]
        for start, one, other, end in zip((HEAT, SALT, EAST, NORTH, WET, PART, MIX), low, high, last):
            if start == MIX and level == LEVELS - 1:
                continue
            row = slice(start + level, start + level + 1)
            a_ref[row] = jnp.where(even, other, one)
            b_ref[row] = jnp.where(even, one, other)
            own_ref[0, row] = one
            own_ref[1, row] = end
    for ref in (a_ref, b_ref):
        ref[MIX + LEVELS - 1 :] = jnp.zeros((PAYLOAD - MIX - LEVELS + 1, COLS), jnp.float32)

    @pl.when(at_top)
    def _():
        back = LANES - 1 - iota((TILE, LANES), 1)
        for row in range(0, PAYLOAD, TILE):
            place = row + iota((TILE, LANES), 0)
            sign = jnp.where(jnp.logical_and(place >= EAST, place < WET), -1.0, 1.0)
            left = b_ref[row : row + TILE, :LANES]
            right = b_ref[row : row + TILE, LANES:]
            flip = lambda x: sign * jnp.take_along_axis(x, back, axis=1, mode="promise_in_bounds")
            b_ref[row : row + TILE, :LANES] = flip(right)
            b_ref[row : row + TILE, LANES:] = flip(left)


def factor(thick, mix, wet):
    inverse, weight, ratio = [], [], []
    for level in range(LEVELS):
        diagonal = thick[level]
        if level < LEVELS - 1:
            weight.append((0.2 * mix[level]) * (wet[level] * wet[level + 1]))
            diagonal = diagonal + weight[level]
        if level > 0:
            diagonal = diagonal + weight[level - 1] * (1.0 - ratio[level - 1])
        inverse.append(1.0 / diagonal)
        if level < LEVELS - 1:
            ratio.append(weight[level] * inverse[level])
    return inverse, weight, ratio


def solve(thick, inverse, weight, ratio, right):
    x = []
    for level in range(LEVELS):
        now = thick[level] * right[level]
        if level > 0:
            now = now + weight[level - 1] * x[level - 1]
        x.append(now * inverse[level])
    for level in reversed(range(LEVELS - 1)):
        x[level] = x[level] + ratio[level] * x[level + 1]
    return x


def pressures(thick, density):
    above, out = None, []
    for level in range(LEVELS):
        layer = (0.1 * thick[level]) * density[level]
        out.append(0.5 * layer if above is None else above + 0.5 * layer)
        above = layer if above is None else above + layer
    return out


def inner_steps(
    thick_ref, spin_ref, heat_ref, salt_ref, east_ref, north_ref, wet_ref, mix_ref,
    heat_out, salt_out, east_out, north_out, inv_out, weight_out, face_e_out, face_n_out, rim_out,
    heat_f, salt_f, east_f, north_f, rim, spins,
):
    thick = [thick_ref[level] for level in range(LEVELS)]
    spins[0:1] = jnp.zeros((1, LANES), jnp.float32)
    spins[0:1, :ROWS] = 0.2 * spin_ref[...]
    spins[...] = jnp.transpose(jnp.broadcast_to(spins[0:1], (LANES, LANES)))
    inner = (iota((TILE, COLS), 1) < COLS - 1).astype(jnp.float32)
    sub = iota((TILE, COLS), 0)
    lane = iota((TILE, LANES), 1)
    for ref in (heat_f, salt_f, east_f, north_f):
        ref[...] = jnp.zeros(ref.shape, jnp.float32)

    def step(block, _):
        rows = tile_rows(block)
        above = tile_rows(jnp.minimum(block + 1, BLOCKS - 1))
        shut = jnp.logical_and(sub == TILE - 1, block == BLOCKS - 1)
        spin = spins[rows]
        spin = jnp.concatenate([spin, spin], axis=1)
        ends = jnp.zeros((TILE, LANES), jnp.float32)
        all_wet, all_mix = [], []
        for level in range(LEVELS):
            pick = lambda ref: (ref[level, rows], north_of(ref[level, rows], ref[level, above], sub))
            heat, heat_n = pick(heat_ref)
            salt, salt_n = pick(salt_ref)
            east, east_n = pick(east_ref)
            north, north_n = pick(north_ref)
            wet, wet_n = (x.astype(jnp.float32) for x in pick(wet_ref))
            all_wet.append(wet)
            both = jnp.where(shut, 0.0, wet * wet_n)
            face_n_out[level, rows] = 0.1 * both
            here, there = weights(both, north + north_n)
            spread = GRAIN * both
            flows = [
                here * heat + there * heat_n,
                here * salt + there * salt_n,
                spread * (east_n - east),
                spread * (north_n - north),
            ]
            change = []
            for ref, flow in zip((heat_f, salt_f, east_f, north_f), flows):
                change.append(flow - south_of(flow, ref[level], sub))
                ref[level] = flow
            coded = jnp.where(wet > 0.0, east, DRY)
            coded_e = east_of(coded)
            both = jnp.where(coded_e < DRY, wet * inner, 0.0)
            face_e_out[level, rows] = 0.1 * both
            here, there = weights(both, coded_e + east)
            spread = GRAIN * both
            flows = [
                here * heat + there * east_of(heat),
                here * salt + there * east_of(salt),
                spread * (coded_e - east),
                spread * (east_of(north) - north),
            ]
            change = [n + (flow - west_of(flow)) for n, flow in zip(change, flows)]
            new_heat = heat - change[0]
            new_salt = salt - change[1]
            heat_out[level, rows] = new_heat
            salt_out[level, rows] = new_salt
            turn = wet * spin
            east_out[level, rows] = east + (turn * north + change[2])
            north_out[level, rows] = north + (change[3] - turn * east)
            fields = [heat, salt, coded, north, mix_down(new_heat, new_salt)]
            if level < LEVELS - 1:
                all_mix.append(mix_ref[level, rows])
                fields.append(all_mix[level])
            for which, x in enumerate(fields):
                place = 2 * (which * LEVELS + level)
                pair = jnp.where(lane == 0, x[:, :LANES], x[:, LANES:])
                pair = pltpu.roll(pair, place + 1, 1)
                ends = jnp.where(jnp.logical_or(lane == place, lane == place + 1), pair, ends)
        rim[rows] = ends
        inverse, weight, _ = factor(thick, all_mix, all_wet)
        for level in range(LEVELS):
            inv_out[level, rows] = inverse[level]
            if level < LEVELS - 1:
                weight_out[level, rows] = weight[level]
        return 0

    lax.fori_loop(0, BLOCKS, step, 0)
    wide = iota((LANES, LANES), 1)
    rim[...] = jnp.where(wide < ROWS, jnp.transpose(rim[...]), 0.0)
    for side, first in ((0, 1), (1, 0)):
        ends = rim[pl.ds(first, ROWS, 2)]
        coded = ends[EAST : EAST + LEVELS]
        rim_out[side, HEAT:EAST] = ends[HEAT:EAST]
        rim_out[side, EAST : EAST + LEVELS] = jnp.where(coded < DRY, coded, 0.0)
        rim_out[side, NORTH : NORTH + LEVELS] = ends[30:40]
        rim_out[side, WET : WET + LEVELS] = jnp.where(coded < DRY, 1.0, 0.0)
        rim_out[side, PART : PART + 2 * LEVELS] = ends[40:60]
        rim_out[side, PART + 2 * LEVELS :] = jnp.zeros((PAYLOAD - PART - 2 * LEVELS, LANES), jnp.float32)


def from_lat(a_ref, b_ref):
    even = lax.axis_index("lat") % 2 == 0
    a, b = a_ref[...], b_ref[...]
    return jnp.where(even, b, a), jnp.where(even, a, b)


def row_faces(hinge_ref, a_ref, b_ref, own_ref, rim_ref, fix_out, rhs_out, c_out, d_out, ghost):
    at_top = lax.axis_index("lat") == lax.axis_size("lat") - 1
    open_north = jnp.where(jnp.logical_and(at_top, hinge_ref[0] == 1), 0.0, 1.0)
    ghost[0], ghost[1] = from_lat(a_ref, b_ref)
    mixed_flux = []
    for side in range(2):
        mine = lambda start: own_ref[side, start : start + LEVELS]
        other = lambda start: ghost[side, start : start + LEVELS]
        low, high = (other, mine) if side == 0 else (mine, other)
        sign = 1.0 if side == 0 else -1.0
        both = low(WET) * high(WET)
        here, there = weights(both, low(NORTH) + high(NORTH))
        spread = -sign * GRAIN * both
        heat_n = here * low(HEAT) + there * high(HEAT)
        salt_n = here * low(SALT) + there * high(SALT)
        changes = (
            sign * heat_n,
            sign * salt_n,
            spread * (high(EAST) - low(EAST)),
            spread * (high(NORTH) - low(NORTH)),
            0.1 * both,
        )
        for which, change in enumerate(changes):
            base = (side * len(changes) + which) * GROUP
            fix_out[base : base + LEVELS] = change
        flux = mix_down(heat_n, salt_n)
        mixed_flux.append(flux)
        change = -flux if side == 0 else open_north * flux
        rhs_out[side * GROUP : side * GROUP + LEVELS] = other(PART) + change
    lane = iota((LEVELS, LANES), 1)
    wide = iota((PAYLOAD, LANES), 1)
    sides = []
    for side, column in ((0, 0), (1, COLS - 1)):
        ends = rim_ref[side]
        for place, which in ((SOUTH_LANE, 0), (NORTH_LANE, 1)):
            ends = jnp.where(wide == place, ghost[which, :, column : column + 1], ends)
        part = rim_ref[side, PART : PART + LEVELS]
        part = part + jnp.where(lane == 0, mixed_flux[0][:, column : column + 1], 0.0)
        part = part - jnp.where(lane == ROWS - 1, mixed_flux[1][:, column : column + 1], 0.0)
        sides.append((ends, part))
    even = lax.axis_index("lon") % 2 == 0
    c_out[...] = jnp.where(even, sides[1][0], sides[0][0])
    d_out[...] = jnp.where(even, sides[0][0], sides[1][0])
    c_out[PART : PART + LEVELS] = jnp.where(even, sides[1][1], sides[0][1])
    d_out[PART : PART + LEVELS] = jnp.where(even, sides[0][1], sides[1][1])


def finish(
    thick_ref, heat_ref, salt_ref, east_ref, north_ref, inv_ref, weight_ref, face_e_ref, face_n_ref,
    a_ref, b_ref, fix_ref, rhs_ref, c_own_ref, d_own_ref, c_ref, d_ref,
    heat_out, salt_out, east_out, north_out,
    heat_x, salt_x, east_x, north_x, press_x, ghost, rims,
    rim_rhs, rim_mix, rim_wet, rim_press, rim_rows, fixes, north_f, sems,
):
    pairs = ((heat_ref, heat_x), (salt_ref, salt_x), (east_ref, east_x), (north_ref, north_x))
    copies = [pltpu.make_async_copy(src, dst, sems.at[i]) for i, (src, dst) in enumerate(pairs)]
    for copy in copies:
        copy.start()
    thick = [thick_ref[level] for level in range(LEVELS)]
    ghost[0], ghost[1] = from_lat(a_ref, b_ref)
    even = lax.axis_index("lon") % 2 == 0
    rims[0] = jnp.where(even, d_own_ref[...], c_own_ref[...])
    rims[1] = jnp.where(even, d_ref[...], c_ref[...])
    rims[2] = jnp.where(even, c_own_ref[...], d_own_ref[...])
    rims[3] = jnp.where(even, c_ref[...], d_ref[...])

    span = lambda which, start: rims[which, start : start + LEVELS]
    lane = iota((LEVELS, LANES), 1)
    mixed_flux = []
    for side, (left, right) in enumerate(((1, 0), (2, 3))):
        both = span(left, WET) * span(right, WET)
        here, there = weights(both, span(left, EAST) + span(right, EAST))
        heat_e = here * span(left, HEAT) + there * span(right, HEAT)
        salt_e = here * span(left, SALT) + there * span(right, SALT)
        own = 1.0 if side == 0 else -1.0
        base = side * ROWS
        fixes[base : base + LEVELS] = own * heat_e
        fixes[base + LEVELS : base + 2 * LEVELS] = own * salt_e
        mixed_flux.append(own * mix_down(heat_e, salt_e))
    rim_rows[0:LEVELS] = span(0, PART) + mixed_flux[0]
    rim_rows[16 : 16 + LEVELS] = span(1, PART) - mixed_flux[0]
    rim_rows[32 : 32 + LEVELS] = span(2, PART) + mixed_flux[1]
    rim_rows[48 : 48 + LEVELS] = span(3, PART) - mixed_flux[1]
    for side, end in ((1, NORTH_LANE), (0, SOUTH_LANE)):
        low = rhs_ref[side * GROUP : side * GROUP + LEVELS, :LANES]
        high = rhs_ref[side * GROUP : side * GROUP + LEVELS, LANES:]
        low = low + jnp.where(lane == 0, mixed_flux[0][:, end : end + 1], 0.0)
        high = high + jnp.where(lane == LANES - 1, mixed_flux[1][:, end : end + 1], 0.0)
        base = 64 + 32 * (1 - side)
        rim_rows[base : base + LEVELS] = low
        rim_rows[base + 16 : base + 16 + LEVELS] = high
    for level in range(LEVELS):
        for slot in range(TILE):
            rim_rhs[level, slot : slot + 1] = rim_rows[16 * slot + level : 16 * slot + level + 1]
            for ref, start in ((rim_mix, MIX), (rim_wet, WET)):
                row = slice(start + level, start + level + 1)
                if slot < 4:
                    value = rims[slot, row]
                else:
                    half = (slot % 2) * LANES
                    value = ghost[1 - (slot - 4) // 2, row, half : half + LANES]
                ref[level, slot : slot + 1] = value
    listed = lambda ref: [ref[level] for level in range(LEVELS)]
    bands = factor(thick, listed(rim_mix), listed(rim_wet))
    rim_density = solve(thick, *bands, listed(rim_rhs))
    for level, value in enumerate(pressures(thick, rim_density)):
        rim_press[level] = value
        for slot in range(TILE):
            rim_rows[16 * slot + level : 16 * slot + level + 1] = rim_press[level, slot : slot + 1]
    for side, (left, right) in enumerate(((1, 0), (2, 3))):
        both = span(left, WET) * span(right, WET)
        own = -1.0 if side == 0 else 1.0
        slope = 0.1 * both * (
            rim_rows[16 * right : 16 * right + LEVELS] - rim_rows[16 * left : 16 * left + LEVELS]
        )
        base = side * ROWS + 2 * LEVELS
        fixes[base : base + LEVELS] = own * GRAIN * both * (span(right, EAST) - span(left, EAST)) - slope
        fixes[base + LEVELS : base + 2 * LEVELS] = own * GRAIN * both * (span(right, NORTH) - span(left, NORTH))
    fixes[...] = jnp.transpose(fixes[...])

    for copy in copies:
        copy.wait()
    for level in range(LEVELS):
        for side, row in ((0, 0), (1, ROWS - 1)):
            for which, ref in enumerate((heat_x, salt_x, east_x, north_x)):
                place = (side * 5 + which) * GROUP + level
                ref[level, row : row + 1] += fix_ref[place : place + 1]
    sub = iota((TILE, COLS), 0)
    lanes = iota((TILE, LANES), 1)

    def fix(corner, which, level):
        place = which * LEVELS + level
        west = jnp.where(lanes == 0, pltpu.roll(corner, (LANES - place) % LANES, 1), 0.0)
        place = place + ROWS
        east = jnp.where(lanes == LANES - 1, pltpu.roll(corner, LANES - 1 - place, 1), 0.0)
        return jnp.concatenate([west, east], axis=1)

    def bands_at(rows):
        inverse = [inv_ref[level, rows] for level in range(LEVELS)]
        weight = [weight_ref[level, rows] for level in range(LEVELS - 1)]
        return inverse, weight, [w * inv for w, inv in zip(weight, inverse)]

    def tracers(block, _):
        rows = tile_rows(block)
        corner = fixes[rows]
        bands = bands_at(rows)
        heat = solve(thick, *bands, [heat_x[level, rows] + fix(corner, 0, level) for level in range(LEVELS)])
        salt = solve(thick, *bands, [salt_x[level, rows] + fix(corner, 1, level) for level in range(LEVELS)])
        density = [mix_down(h, s) for h, s in zip(heat, salt)]
        for level, value in enumerate(pressures(thick, density)):
            heat_out[level, rows] = heat[level]
            salt_out[level, rows] = salt[level]
            press_x[level, rows] = value
        return 0

    lax.fori_loop(0, BLOCKS, tracers, 0)

    for level in range(LEVELS):
        north_f[level] = jnp.zeros((TILE, COLS), jnp.float32)
        for side, row in ((0, 0), (1, ROWS - 1)):
            place = (side * 5 + 4) * GROUP + level
            slot = 16 * (6 - 2 * side) + level
            outer = jnp.concatenate([rim_rows[slot : slot + 1], rim_rows[slot + 16 : slot + 17]], axis=1)
            slope = fix_ref[place : place + 1] * (press_x[level, row : row + 1] - outer)
            north_x[level, row : row + 1] += slope if side == 1 else -slope

    def flow(block, _):
        rows = tile_rows(block)
        above = tile_rows(jnp.minimum(block + 1, BLOCKS - 1))
        corner = fixes[rows]
        new_east, new_north = [], []
        for level in range(LEVELS):
            press = press_x[level, rows]
            press_n = north_of(press, press_x[level, above], sub)
            slope_n = face_n_ref[level, rows] * (press_n - press)
            slope_s = south_of(slope_n, north_f[level], sub)
            north_f[level] = slope_n
            slope_e = face_e_ref[level, rows] * (east_of(press) - press)
            new_east.append(east_x[level, rows] - (slope_e + west_of(slope_e)) + fix(corner, 2, level))
            new_north.append(north_x[level, rows] - (slope_n + slope_s) + fix(corner, 3, level))
        bands = bands_at(rows)
        for out, right in ((east_out, new_east), (north_out, new_north)):
            for level, value in enumerate(solve(thick, *bands, right)):
                out[level, rows] = value
        return 0

    lax.fori_loop(0, BLOCKS, flow, 0)


def swap_in_pairs(x, axis, first):
    count = lax.axis_size(axis)
    return lax.ppermute(x, axis, [(i, (((i - first) ^ 1) + first) % count) for i in range(count)])


def swap_with_fold(x, anchor):
    lon, lat = lax.axis_size("lon"), lax.axis_size("lat")
    pairs = []
    for i in range(lon):
        for j in range(1, lat - 1):
            pairs.append((i * lat + j, i * lat + ((j - 1) ^ 1) + 1))
        pairs.append((i * lat + lat - 1, (anchor - 1 - i) % lon * lat + lat - 1))
    return lax.ppermute(x, ("lon", "lat"), pairs)


SMEM = pl.BlockSpec(memory_space=pltpu.SMEM)
VMEM = pl.BlockSpec(memory_space=pltpu.VMEM)
ANYWHERE = pl.BlockSpec(memory_space=pl.ANY)


def small(*shape):
    return pltpu.VMEM(shape, jnp.float32)


def made(*shape):
    return jax.ShapeDtypeStruct(shape, jnp.float32)


PLAIN = (LEVELS, ROWS, COLS)
LESS = (LEVELS - 1, ROWS, COLS)
CARRY = (LEVELS, TILE, COLS)
RIM = (LEVELS, TILE, LANES)


def inner_beside_rows(anchor, a_sent, b_sent, cells, spacing, spin):
    b_got = swap_with_fold(b_sent, anchor)
    a_got = swap_in_pairs(a_sent, "lat", 0)
    *steps, rim = pl.pallas_call(
        inner_steps,
        in_specs=[SMEM] + [VMEM] * 7,
        out_specs=[VMEM] * 9,
        out_shape=[made(*PLAIN)] * 5 + [made(*LESS)] + [made(*PLAIN)] * 2 + [made(2, PAYLOAD, LANES)],
        scratch_shapes=[small(*CARRY)] * 4 + [small(LANES, LANES)] * 2,
        cost_estimate=pl.CostEstimate(flops=25 * 10**6, bytes_accessed=12 * 10**6, transcendentals=0),
        compiler_params=pltpu.CompilerParams(vmem_limit_bytes=16 * 2**20),
        name="inner_steps",
    )(spacing, spin, *cells)
    return a_got, b_got, steps, rim


def columns_and_finish(a_got, b_got, steps, rim, own, spacing, hinge):
    fix, rhs, c_sent, d_sent = pl.pallas_call(
        row_faces,
        in_specs=[SMEM] + [VMEM] * 4,
        out_specs=[VMEM] * 4,
        out_shape=[made(10 * GROUP, COLS), made(2 * GROUP, COLS)] + [made(PAYLOAD, LANES)] * 2,
        scratch_shapes=[small(2, PAYLOAD, COLS)],
        compiler_params=pltpu.CompilerParams(vmem_limit_bytes=4 * 2**20),
        name="row_faces",
    )(hinge, a_got, b_got, own, rim)
    d_got = swap_in_pairs(d_sent, "lon", 1)
    c_got = swap_in_pairs(c_sent, "lon", 0)
    return pl.pallas_call(
        finish,
        in_specs=[SMEM] + [ANYWHERE] * 4 + [VMEM] * 12,
        out_specs=[VMEM] * 4,
        out_shape=[made(*PLAIN)] * 4,
        scratch_shapes=[small(*PLAIN)] * 5
        + [small(2, PAYLOAD, COLS), small(4, PAYLOAD, LANES)]
        + [small(*RIM)] * 4
        + [small(LANES, LANES)] * 2
        + [small(*CARRY), pltpu.SemaphoreType.DMA((4,))],
        compiler_params=pltpu.CompilerParams(vmem_limit_bytes=16 * 2**20),
        name="finish",
    )(spacing, *steps, a_got, b_got, fix, rhs, c_sent, d_sent, c_got, d_got)


def on_device(heat, salt, east, north, marine, mixing, spacing, spin, hinge, partner):
    lon = lax.axis_size("lon")
    anchor = (partner[0] + 1 + COLS * lax.axis_index("lon")) // COLS % lon
    cells = (heat, salt, east, north, marine, mixing)
    edge = [
        pl.BlockSpec((x.shape[0], TILE, COLS), lambda i, at=at: (0, at, 0))
        for at in (0, BLOCKS - 1)
        for x in cells
    ]
    payload = pl.BlockSpec((PAYLOAD, COLS), lambda i: (0, 0))
    a_sent, b_sent, own = pl.pallas_call(
        pack_rows,
        grid=(1,),
        in_specs=[SMEM] + edge,
        out_specs=[payload] * 2 + [pl.BlockSpec((2, PAYLOAD, COLS), lambda i: (0, 0, 0))],
        out_shape=[made(PAYLOAD, COLS)] * 2 + [made(2, PAYLOAD, COLS)],
        compiler_params=pltpu.CompilerParams(vmem_limit_bytes=8 * 2**20),
        name="pack_rows",
    )(hinge, *cells, *cells)
    branches = [functools.partial(inner_beside_rows, k) for k in range(lon)]
    got = lax.switch(anchor, branches, a_sent, b_sent, cells, spacing, spin.reshape(1, -1))
    return columns_and_finish(*got, own, spacing, hinge)


def solution(mesh):
    cells = P(None, "lat", "lon")
    return jax.shard_map(
        on_device,
        mesh=mesh,
        in_specs=(cells,) * 6 + (P(), P("lat"), P(), P("lon")),
        out_specs=(cells,) * 4,
        check_vma=False,
    )
```

```python
import functools

import jax
import jax.numpy as jnp
from jax import lax
from jax.experimental import pallas as pl
from jax.experimental.pallas import tpu as pltpu
from jax.sharding import PartitionSpec as P

LEVELS = 10
ROWS = 64
COLS = 256
TILE = 8
BLOCKS = ROWS // TILE
LANES = 128
GROUP = 16
HEAT, SALT, EAST, NORTH, WET, PART, MIX = 0, 10, 20, 30, 40, 50, 60
PAYLOAD = 72
SOUTH_LANE, NORTH_LANE = 64, 65
GRAIN = 0.06
OPEN_NORTH = 16
DRY = 1.0e30


def iota(shape, dim):
    return lax.broadcasted_iota(jnp.int32, shape, dim)


def weights(both, speeds):
    speed = 0.1 * speeds
    return both * (jnp.maximum(speed, 0.0) + GRAIN), both * (jnp.minimum(speed, 0.0) - GRAIN)


def east_of(x):
    return pltpu.roll(x, x.shape[1] - 1, 1)


def west_of(x):
    return pltpu.roll(x, 1, 1)


def north_of(x, block_above, sub):
    return pltpu.roll(jnp.where(sub == 0, block_above, x), TILE - 1, 0)


def south_of(x, block_below, sub):
    return pltpu.roll(jnp.where(sub == TILE - 1, block_below, x), 1, 0)


def mix_down(heat, salt):
    return 0.8 * salt - 0.2 * heat


def tile_rows(block):
    return pl.ds(pl.multiple_of(block * TILE, TILE), TILE)


def pack_rows(
    hinge_hbm, partner_hbm, thick_hbm, spin_hbm,
    heat_hbm, salt_hbm, east_hbm, north_hbm, wet_hbm, mix_hbm,
    anchor_ref, a_ref, b_ref, own_ref, const_ref, spins_ref,
    heat_in, salt_in, east_in, north_in, wet_in, mix_in,
    hinge_ref, partner_ref, thick_ref, spin_ref,
    heat_e, salt_e, east_e, north_e, wet_e, mix_e, sems,
):
    sources = (heat_hbm, salt_hbm, east_hbm, north_hbm, wet_hbm, mix_hbm)
    edges = (heat_e, salt_e, east_e, north_e, wet_e, mix_e)
    pairs = [(hinge_hbm, hinge_ref), (partner_hbm, partner_ref), (thick_hbm, thick_ref), (spin_hbm, spin_ref)]
    for side, first in ((0, 0), (1, ROWS - TILE)):
        pairs += [(src.at[:, pl.ds(first, TILE)], dst.at[side]) for src, dst in zip(sources, edges)]
    early = len(pairs)
    pairs += zip(sources, (heat_in, salt_in, east_in, north_in, wet_in, mix_in))
    copies = [pltpu.make_async_copy(src, dst, sems.at[i]) for i, (src, dst) in enumerate(pairs)]
    for copy in copies:
        copy.start()
    for copy in copies[:early]:
        copy.wait()
    lon = lax.axis_size("lon")
    anchor_ref[0] = (partner_ref[0] + 1 + COLS * lax.axis_index("lon")) // COLS % lon
    for level in range(LEVELS):
        const_ref[level : level + 1] = jnp.full((1, COLS), thick_ref[level], jnp.float32)
    spins_ref[0:1] = jnp.zeros((1, LANES), jnp.float32)
    spins_ref[0:1, :ROWS] = 0.2 * spin_ref[...]
    spins_ref[...] = jnp.transpose(jnp.broadcast_to(spins_ref[0:1], (LANES, LANES)))
    bottom, top = ([ref.at[side] for ref in edges] for side in range(2))
    lat = lax.axis_index("lat")
    at_top = lat == lax.axis_size("lat") - 1
    even = lat % 2 == 0
    hinged = jnp.logical_and(at_top, hinge_ref[0] == 1)
    const_ref[OPEN_NORTH : OPEN_NORTH + 1] = jnp.full((1, COLS), jnp.where(hinged, 0.0, 1.0), jnp.float32)
    inner = (iota((TILE, COLS), 1) < COLS - 1).astype(jnp.float32)
    sub = iota((TILE, COLS), 0)
    for level in range(LEVELS):
        sides = []
        for heat_ref, salt_ref, east_ref, north_ref, wet_ref, mix_ref in (bottom, top):
            heat, salt = heat_ref[level], salt_ref[level]
            east, north = east_ref[level], north_ref[level]
            wet = wet_ref[level].astype(jnp.float32)
            mixed = mix_down(heat, salt)
            here, there = weights(wet * inner * east_of(wet), east + east_of(east))
            flux_e = here * mixed + there * east_of(mixed)
            above = lambda x: pltpu.roll(x, TILE - 1, 0)
            here, there = weights(wet * above(wet), north + above(north))
            flux_n = here * mixed + there * above(mixed)
            part = mixed - (flux_e - west_of(flux_e))
            sides.append((heat, salt, east, north, wet, part, mix_ref[min(level, LEVELS - 2)], flux_n))
        *low, flux_n = sides[0]
        low[5] = low[5] - flux_n
        low = [x[:1] for x in low]
        *high, flux_n = sides[1]
        flux_s = pltpu.roll(flux_n, 1, 0)
        high[5] = high[5] + flux_s - jnp.where(sub == TILE - 1, 0.0, flux_n)
        last = [x[TILE - 1 :] for x in high]
        high = [jnp.where(hinged, x[TILE - 2 : TILE - 1], end) for x, end in zip(high, last)]
        for start, one, other, end in zip((HEAT, SALT, EAST, NORTH, WET, PART, MIX), low, high, last):
            if start == MIX and level == LEVELS - 1:
                continue
            row = slice(start + level, start + level + 1)
            a_ref[row] = jnp.where(even, other, one)
            b_ref[row] = jnp.where(even, one, other)
            own_ref[0, row] = one
            own_ref[1, row] = end
    for ref in (a_ref, b_ref):
        ref[MIX + LEVELS - 1 :] = jnp.zeros((PAYLOAD - MIX - LEVELS + 1, COLS), jnp.float32)

    @pl.when(at_top)
    def _():
        back = LANES - 1 - iota((TILE, LANES), 1)
        for row in range(0, PAYLOAD, TILE):
            place = row + iota((TILE, LANES), 0)
            sign = jnp.where(jnp.logical_and(place >= EAST, place < WET), -1.0, 1.0)
            left = b_ref[row : row + TILE, :LANES]
            right = b_ref[row : row + TILE, LANES:]
            flip = lambda x: sign * jnp.take_along_axis(x, back, axis=1, mode="promise_in_bounds")
            b_ref[row : row + TILE, :LANES] = flip(right)
            b_ref[row : row + TILE, LANES:] = flip(left)

    for copy in copies[early:]:
        copy.wait()


def factor(thick, mix, wet):
    inverse, weight, ratio = [], [], []
    for level in range(LEVELS):
        diagonal = thick[level]
        if level < LEVELS - 1:
            weight.append((0.2 * mix[level]) * (wet[level] * wet[level + 1]))
            diagonal = diagonal + weight[level]
        if level > 0:
            diagonal = diagonal + weight[level - 1] * (1.0 - ratio[level - 1])
        inverse.append(1.0 / diagonal)
        if level < LEVELS - 1:
            ratio.append(weight[level] * inverse[level])
    return inverse, weight, ratio


def solve(thick, inverse, weight, ratio, right):
    x = []
    for level in range(LEVELS):
        now = thick[level] * right[level]
        if level > 0:
            now = now + weight[level - 1] * x[level - 1]
        x.append(now * inverse[level])
    for level in reversed(range(LEVELS - 1)):
        x[level] = x[level] + ratio[level] * x[level + 1]
    return x


def pressures(thick, density):
    above, out = None, []
    for level in range(LEVELS):
        layer = (0.1 * thick[level]) * density[level]
        out.append(0.5 * layer if above is None else above + 0.5 * layer)
        above = layer if above is None else above + layer
    return out


def thicknesses(const_ref, width):
    return [const_ref[level : level + 1, :width] for level in range(LEVELS)]


def inner_steps(
    const_ref, spins, heat_ref, salt_ref, east_ref, north_ref, wet_ref, mix_ref,
    heat_out, salt_out, east_out, north_out, inv_out, weight_out, face_e_out, face_n_out, rim_out, rim_face_out,
    heat_f, salt_f, east_f, north_f, rim, rim_face,
):
    thick = thicknesses(const_ref, COLS)
    inner = (iota((TILE, COLS), 1) < COLS - 1).astype(jnp.float32)
    sub = iota((TILE, COLS), 0)
    lane = iota((TILE, LANES), 1)
    for ref in (heat_f, salt_f, east_f, north_f):
        ref[...] = jnp.zeros(ref.shape, jnp.float32)

    def step(block, _):
        rows = tile_rows(block)
        above = tile_rows(jnp.minimum(block + 1, BLOCKS - 1))
        shut = jnp.logical_and(sub == TILE - 1, block == BLOCKS - 1)
        spin = spins[rows]
        spin = jnp.concatenate([spin, spin], axis=1)
        ends = jnp.zeros((TILE, LANES), jnp.float32)
        end_faces = ends
        all_wet, all_mix = [], []
        stack = lambda ref: ref[:, rows].reshape(LEVELS * TILE, COLS)
        heat_all, salt_all, north_all = (east_of(stack(ref)) for ref in (heat_ref, salt_ref, north_ref))
        coded_all = jnp.where(stack(wet_ref) > 0, stack(east_ref), DRY)
        coded_east = east_of(coded_all)
        for level in range(LEVELS):
            mine = slice(level * TILE, level * TILE + TILE)
            pick = lambda ref: (ref[level, rows], north_of(ref[level, rows], ref[level, above], sub))
            heat, heat_n = pick(heat_ref)
            salt, salt_n = pick(salt_ref)
            east, east_n = pick(east_ref)
            north, north_n = pick(north_ref)
            wet, wet_n = (x.astype(jnp.float32) for x in pick(wet_ref))
            all_wet.append(wet)
            both = jnp.where(shut, 0.0, wet * wet_n)
            face_n_out[level, rows] = 0.1 * both
            here, there = weights(both, north + north_n)
            spread = GRAIN * both
            flows = [
                here * heat + there * heat_n,
                here * salt + there * salt_n,
                spread * (east_n - east),
                spread * (north_n - north),
            ]
            change = []
            for ref, flow in zip((heat_f, salt_f, east_f, north_f), flows):
                change.append(flow - south_of(flow, ref[level], sub))
                ref[level] = flow
            coded, coded_e = coded_all[mine], coded_east[mine]
            both = jnp.where(coded_e < 0.5 * DRY, wet * inner, 0.0)
            face = 0.1 * both
            face_e_out[level, rows] = face
            place = 4 * level
            pair = pltpu.roll(jnp.where(lane == 0, face[:, :LANES], face[:, LANES:]), place + 2, 1)
            end_faces = jnp.where(jnp.logical_or(lane == place, lane == place + 2), pair, end_faces)
            here, there = weights(both, coded_e + east)
            spread = GRAIN * both
            flows = [
                here * heat + there * heat_all[mine],
                here * salt + there * salt_all[mine],
                spread * (coded_e - east),
                spread * (north_all[mine] - north),
            ]
            change = [n + (flow - west_of(flow)) for n, flow in zip(change, flows)]
            new_heat = heat - change[0]
            new_salt = salt - change[1]
            heat_out[level, rows] = new_heat
            salt_out[level, rows] = new_salt
            turn = wet * spin
            east_out[level, rows] = east + (turn * north + change[2])
            north_out[level, rows] = north + (change[3] - turn * east)
            fields = [heat, salt, coded, north, mix_down(new_heat, new_salt)]
            if level < LEVELS - 1:
                all_mix.append(mix_ref[level, rows])
                fields.append(all_mix[level])
            for which, x in enumerate(fields):
                place = 2 * (which * LEVELS + level)
                pair = jnp.where(lane == 0, x[:, :LANES], x[:, LANES:])
                pair = pltpu.roll(pair, place + 1, 1)
                ends = jnp.where(jnp.logical_or(lane == place, lane == place + 1), pair, ends)
        rim[rows] = ends
        rim_face[rows] = end_faces
        inverse, weight, _ = factor(thick, all_mix, all_wet)
        for level in range(LEVELS):
            inv_out[level, rows] = inverse[level]
            if level < LEVELS - 1:
                weight_out[level, rows] = weight[level]
        return 0

    lax.fori_loop(0, BLOCKS, step, 0)
    wide = iota((LANES, LANES), 1)
    rim[...] = jnp.where(wide < ROWS, jnp.transpose(rim[...]), 0.0)
    rim_face[...] = jnp.where(wide < ROWS, jnp.transpose(rim_face[...]), 0.0)
    for side, first in ((0, 1), (1, 0)):
        rim_face_out[side, :LEVELS] = rim_face[pl.ds(2 * first, LEVELS, 4)]
        ends = rim[pl.ds(first, ROWS, 2)]
        coded = ends[EAST : EAST + LEVELS]
        rim_out[side, HEAT:EAST] = ends[HEAT:EAST]
        rim_out[side, EAST : EAST + LEVELS] = jnp.where(coded < DRY, coded, 0.0)
        rim_out[side, NORTH : NORTH + LEVELS] = ends[30:40]
        rim_out[side, WET : WET + LEVELS] = jnp.where(coded < DRY, 1.0, 0.0)
        rim_out[side, PART : PART + 2 * LEVELS] = ends[40:60]
        rim_out[side, PART + 2 * LEVELS :] = jnp.zeros((PAYLOAD - PART - 2 * LEVELS, LANES), jnp.float32)


def from_lat(a_ref, b_ref):
    even = lax.axis_index("lat") % 2 == 0
    a, b = a_ref[...], b_ref[...]
    return jnp.where(even, b, a), jnp.where(even, a, b)


def row_faces(const_ref, a_ref, b_ref, own_ref, rim_ref, fix_out, rhs_out, c_out, d_out, ghost):
    open_north = const_ref[OPEN_NORTH : OPEN_NORTH + 1]
    ghost[0], ghost[1] = from_lat(a_ref, b_ref)
    mixed_flux = []
    for side in range(2):
        mine = lambda start: own_ref[side, start : start + LEVELS]
        other = lambda start: ghost[side, start : start + LEVELS]
        low, high = (other, mine) if side == 0 else (mine, other)
        sign = 1.0 if side == 0 else -1.0
        both = low(WET) * high(WET)
        here, there = weights(both, low(NORTH) + high(NORTH))
        spread = -sign * GRAIN * both
        heat_n = here * low(HEAT) + there * high(HEAT)
        salt_n = here * low(SALT) + there * high(SALT)
        changes = (
            sign * heat_n,
            sign * salt_n,
            spread * (high(EAST) - low(EAST)),
            spread * (high(NORTH) - low(NORTH)),
            0.1 * both,
        )
        for which, change in enumerate(changes):
            base = (side * len(changes) + which) * GROUP
            fix_out[base : base + LEVELS] = change
        flux = mix_down(heat_n, salt_n)
        mixed_flux.append(flux)
        change = -flux if side == 0 else open_north * flux
        rhs_out[side * GROUP : side * GROUP + LEVELS] = other(PART) + change
    lane = iota((LEVELS, LANES), 1)
    wide = iota((PAYLOAD, LANES), 1)
    sides = []
    for side, column in ((0, 0), (1, COLS - 1)):
        ends = rim_ref[side]
        for place, which in ((SOUTH_LANE, 0), (NORTH_LANE, 1)):
            ends = jnp.where(wide == place, ghost[which, :, column : column + 1], ends)
        part = rim_ref[side, PART : PART + LEVELS]
        part = part + jnp.where(lane == 0, mixed_flux[0][:, column : column + 1], 0.0)
        part = part - jnp.where(lane == ROWS - 1, mixed_flux[1][:, column : column + 1], 0.0)
        sides.append((ends, part))
    even = lax.axis_index("lon") % 2 == 0
    c_out[...] = jnp.where(even, sides[1][0], sides[0][0])
    d_out[...] = jnp.where(even, sides[0][0], sides[1][0])
    c_out[PART : PART + LEVELS] = jnp.where(even, sides[1][1], sides[0][1])
    d_out[PART : PART + LEVELS] = jnp.where(even, sides[0][1], sides[1][1])


def bands_at(inv_ref, weight_ref, rows):
    inverse = [inv_ref[level, rows] for level in range(LEVELS)]
    weight = [weight_ref[level, rows] for level in range(LEVELS - 1)]
    return inverse, weight, [w * inv for w, inv in zip(weight, inverse)]


def settle(
    const_ref, heat_ref, salt_ref, east_ref, north_ref, inv_ref, weight_ref, face_e_ref, face_n_ref,
    ghost, fix_ref, rhs_ref,
    heat_out, salt_out, east_out, north_out,
    press_x, rim_rhs, rim_mix, rim_wet, rim_press, north_f, outer_p,
):
    for level in range(LEVELS):
        for slot in range(TILE):
            side, half = slot // 2 % 2, slot % 2 * LANES
            row = side * GROUP + level
            rim_rhs[level, slot : slot + 1] = rhs_ref[row : row + 1, half : half + LANES]
            for ref, start in ((rim_mix, MIX), (rim_wet, WET)):
                row = start + level
                ref[level, slot : slot + 1] = ghost[side, row : row + 1, half : half + LANES]
    listed = lambda ref: [ref[level] for level in range(LEVELS)]
    thin = thicknesses(const_ref, LANES)
    rim_density = solve(thin, *(bands := factor(thin, listed(rim_mix), listed(rim_wet))), listed(rim_rhs))
    for level, value in enumerate(pressures(thin, rim_density)):
        rim_press[level] = value
        for slot in range(4):
            half = slot % 2 * LANES
            outer_p[slot // 2, level : level + 1, half : half + LANES] = rim_press[level, slot : slot + 1]

    for level in range(LEVELS):
        for side, row in ((0, 0), (1, ROWS - 1)):
            for which, (src, out) in enumerate(
                ((heat_ref, heat_out), (salt_ref, salt_out), (east_ref, east_out), (north_ref, north_out))
            ):
                place = (side * 5 + which) * GROUP + level
                out[level, row : row + 1] = src[level, row : row + 1] + fix_ref[place : place + 1]
    thick = thicknesses(const_ref, COLS)
    sub = iota((TILE, COLS), 0)

    def tracers(block, _):
        rows = tile_rows(block)
        bands = bands_at(inv_ref, weight_ref, rows)
        first = jnp.logical_and(block == 0, sub == 0)
        last = jnp.logical_and(block == BLOCKS - 1, sub == TILE - 1)
        fixed = jnp.logical_or(first, last)
        take = lambda src, out: [jnp.where(fixed, out[level, rows], src[level, rows]) for level in range(LEVELS)]
        heat = solve(thick, *bands, take(heat_ref, heat_out))
        salt = solve(thick, *bands, take(salt_ref, salt_out))
        density = [mix_down(h, s) for h, s in zip(heat, salt)]
        for level, value in enumerate(pressures(thick, density)):
            heat_out[level, rows] = heat[level]
            salt_out[level, rows] = salt[level]
            press_x[level, rows] = value
        return 0

    lax.fori_loop(0, BLOCKS, tracers, 0)
    for level in range(LEVELS):
        north_f[level] = jnp.zeros((TILE, COLS), jnp.float32)
        for side, row in ((0, 0), (1, ROWS - 1)):
            place = (side * 5 + 4) * GROUP + level
            outer = outer_p[side, level : level + 1]
            slope = fix_ref[place : place + 1] * (press_x[level, row : row + 1] - outer)
            north_out[level, row : row + 1] += slope if side == 1 else -slope

    def flow(block, _):
        rows = tile_rows(block)
        above = tile_rows(jnp.minimum(block + 1, BLOCKS - 1))
        first = jnp.logical_and(block == 0, sub == 0)
        last = jnp.logical_and(block == BLOCKS - 1, sub == TILE - 1)
        fixed = jnp.logical_or(first, last)
        for level in range(LEVELS):
            press = press_x[level, rows]
            press_n = north_of(press, press_x[level, above], sub)
            slope_n = face_n_ref[level, rows] * (press_n - press)
            slope_s = south_of(slope_n, north_f[level], sub)
            north_f[level] = slope_n
            slope_e = face_e_ref[level, rows] * (east_of(press) - press)
            east = jnp.where(fixed, east_out[level, rows], east_ref[level, rows])
            north = jnp.where(fixed, north_out[level, rows], north_ref[level, rows])
            east_out[level, rows] = east - (slope_e + west_of(slope_e))
            north_out[level, rows] = north - (slope_n + slope_s)
        return 0

    lax.fori_loop(0, BLOCKS, flow, 0)


def row_shifts(x, lane):
    after = jnp.where(lane == ROWS, pltpu.roll(x, LANES - 1, 1), x)
    before = jnp.where(lane == LANES - 1, pltpu.roll(x, LANES - 1 - SOUTH_LANE, 1), x)
    return pltpu.roll(after, LANES - 1, 1), pltpu.roll(before, 1, 1)


def finish(
    const_ref, heat_ref, salt_ref, east_ref, north_ref, inv_ref, weight_ref, rim_face_ref,
    c_own_ref, d_own_ref, c_ref, d_ref,
    heat_out, salt_out, east_out, north_out,
    rims, rim_rhs, rim_mix, rim_wet, rim_rows, fixes, heat_x, salt_x, east_x, north_x, sems,
):
    even = lax.axis_index("lon") % 2 == 0
    rims[0] = jnp.where(even, d_own_ref[...], c_own_ref[...])
    rims[1] = jnp.where(even, d_ref[...], c_ref[...])
    rims[2] = jnp.where(even, c_own_ref[...], d_own_ref[...])
    rims[3] = jnp.where(even, c_ref[...], d_ref[...])
    span = lambda which, start: rims[which, start : start + LEVELS]
    slots = lambda slot: slice(GROUP * slot, GROUP * slot + LEVELS)
    lane = iota((LEVELS, LANES), 1)
    sides = ((1, 0), (2, 3))
    for side, (left, right) in enumerate(sides):
        both = span(left, WET) * span(right, WET)
        here, there = weights(both, span(left, EAST) + span(right, EAST))
        heat_e = here * span(left, HEAT) + there * span(right, HEAT)
        salt_e = here * span(left, SALT) + there * span(right, SALT)
        own = 1.0 if side == 0 else -1.0
        rim_rows[slots(2 * side)] = own * heat_e
        rim_rows[slots(2 * side + 1)] = own * salt_e
        rim_rows[slots(4 + side)] = span(2 * side + 1, PART) - own * mix_down(heat_e, salt_e)
        rim_rows[slots(6 + side)] = span(2 * side, PART)
    source = (0, 0, 2, 2, 1, 3, 0, 2)
    for level in range(LEVELS):
        for slot in range(TILE):
            rim_rhs[level, slot : slot + 1] = rim_rows[GROUP * slot + level : GROUP * slot + level + 1]
            for ref, start in ((rim_mix, MIX), (rim_wet, WET)):
                ref[level, slot : slot + 1] = rims[source[slot], start + level : start + level + 1]
    listed = lambda ref: [ref[level] for level in range(LEVELS)]
    thin = thicknesses(const_ref, LANES)
    solved = solve(thin, *factor(thin, listed(rim_mix), listed(rim_wet)), listed(rim_rhs))
    for level, value in enumerate(solved):
        rim_rhs[level] = value
        for slot in range(TILE):
            rim_rows[GROUP * slot + level : GROUP * slot + level + 1] = rim_rhs[level, slot : slot + 1]

    def pressed(density):
        out = pressures(thin, [density[level : level + 1] for level in range(LEVELS)])
        return jnp.concatenate(out, axis=0)

    for side, (left, right) in enumerate(sides):
        heat, salt = rim_rows[slots(2 * side)], rim_rows[slots(2 * side + 1)]
        change = pressed(mix_down(heat, salt))
        mine = pressed(rim_rows[slots(6 + side)]) + change
        other = pressed(rim_rows[slots(4 + side)])
        low, high = (other, mine) if side == 0 else (mine, other)
        both = span(left, WET) * span(right, WET)
        own = -1.0 if side == 0 else 1.0
        slope = 0.1 * both * (high - low)
        inner = rim_face_ref[side, :LEVELS] * change
        inner = inner if side == 0 else -inner
        wet = span(2 * side, WET)
        wet_n, wet_s = row_shifts(wet, lane)
        change_n, change_s = row_shifts(change, lane)
        pull = 0.1 * (wet * wet_n * (change_n - change) + wet * wet_s * (change - change_s))
        east = own * GRAIN * both * (span(right, EAST) - span(left, EAST)) - slope + inner
        north = own * GRAIN * both * (span(right, NORTH) - span(left, NORTH)) - pull
        west_side = 1 - side
        fixes[pl.ds(1 + west_side, LEVELS, 4)] = east
        fixes[pl.ds(3 * west_side, LEVELS, 4)] = inner
        for which, value in enumerate((heat, salt, north)):
            fixes[pl.ds(40 + 20 * which + west_side, LEVELS, 2)] = value
    fixes[...] = jnp.transpose(fixes[...])
    thick = thicknesses(const_ref, COLS)
    lanes = iota((TILE, LANES), 1)

    def fix(corner, place, reach):
        turned = pltpu.roll(corner, LANES - place, 1)
        west = jnp.where(lanes < reach, turned, 0.0)
        east = jnp.where(lanes >= LANES - reach, turned, 0.0)
        return jnp.concatenate([west, east], axis=1)

    def leave(block):
        rows = tile_rows(block)
        pairs = ((heat_x, heat_out), (salt_x, salt_out), (east_x, east_out), (north_x, north_out))
        return [
            pltpu.make_async_copy(src.at[:, rows], dst.at[:, rows], sems.at[block, i])
            for i, (src, dst) in enumerate(pairs)
        ]

    def flow(block, _):
        rows = tile_rows(block)
        corner = fixes[rows]
        new_east, new_north = [], []
        for level in range(LEVELS):
            heat_x[level, rows] = heat_ref[level, rows] + fix(corner, 41 + 2 * level, 1)
            salt_x[level, rows] = salt_ref[level, rows] + fix(corner, 61 + 2 * level, 1)
            new_east.append(east_ref[level, rows] + fix(corner, 4 * level + 2, 2))
            new_north.append(north_ref[level, rows] + fix(corner, 81 + 2 * level, 1))
        bands = bands_at(inv_ref, weight_ref, rows)
        for out, right in ((east_x, new_east), (north_x, new_north)):
            for level, value in enumerate(solve(thick, *bands, right)):
                out[level, rows] = value
        for copy in leave(block):
            copy.start()
        return 0

    lax.fori_loop(0, BLOCKS, flow, 0)
    for block in range(BLOCKS):
        for copy in leave(block):
            copy.wait()


def swap_in_pairs(x, axis, first):
    count = lax.axis_size(axis)
    return lax.ppermute(x, axis, [(i, (((i - first) ^ 1) + first) % count) for i in range(count)])


def swap_with_fold(x, anchor):
    lon, lat = lax.axis_size("lon"), lax.axis_size("lat")
    pairs = []
    for i in range(lon):
        for j in range(1, lat - 1):
            pairs.append((i * lat + j, i * lat + ((j - 1) ^ 1) + 1))
        pairs.append((i * lat + lat - 1, (anchor - 1 - i) % lon * lat + lat - 1))
    return lax.ppermute(x, ("lon", "lat"), pairs)


SMEM = pl.BlockSpec(memory_space=pltpu.SMEM)
VMEM = pl.BlockSpec(memory_space=pltpu.VMEM)
ANYWHERE = pl.BlockSpec(memory_space=pl.ANY)


def small(*shape):
    return pltpu.VMEM(shape, jnp.float32)


def made(*shape):
    return jax.ShapeDtypeStruct(shape, jnp.float32)


PLAIN = (LEVELS, ROWS, COLS)
LESS = (LEVELS - 1, ROWS, COLS)
CARRY = (LEVELS, TILE, COLS)
RIM = (LEVELS, TILE, LANES)


def limit(mib):
    return pltpu.CompilerParams(vmem_limit_bytes=mib * 2**20)


def cost(micros):
    return pl.CostEstimate(flops=0, bytes_accessed=int(micros * 3.5e6), transcendentals=0)


def inner_beside_rows(anchor, a_sent, b_sent, own, const, spins, cells):
    b_got = swap_with_fold(b_sent, anchor)
    a_got = swap_in_pairs(a_sent, "lat", 0)
    *steps, rim, rim_face = pl.pallas_call(
        inner_steps,
        in_specs=[VMEM] * 8,
        out_specs=[VMEM] * 10,
        out_shape=[made(*PLAIN)] * 5 + [made(*LESS)] + [made(*PLAIN)] * 2
        + [made(2, PAYLOAD, LANES), made(2, GROUP, LANES)],
        scratch_shapes=[small(*CARRY)] * 4 + [small(LANES, LANES)] * 2,
        cost_estimate=cost(5),
        compiler_params=limit(16),
        name="inner_steps",
    )(const, spins, *cells)
    faces = pl.pallas_call(
        row_faces,
        in_specs=[VMEM] * 5,
        out_specs=[VMEM] * 5,
        out_shape=[made(10 * GROUP, COLS), made(2 * GROUP, COLS)] + [made(PAYLOAD, LANES)] * 2
        + [made(2, PAYLOAD, COLS)],
        cost_estimate=cost(0.5),
        compiler_params=limit(4),
        name="row_faces",
    )(const, a_got, b_got, own, rim)
    return faces, steps, rim_face


def columns_and_finish(faces, steps, rim_face, const):
    fix, rhs, c_sent, d_sent, ghost = faces
    d_got = swap_in_pairs(d_sent, "lon", 1)
    c_got = swap_in_pairs(c_sent, "lon", 0)
    *steps, inverse, weight, face_e, face_n = steps
    steps = pl.pallas_call(
        settle,
        in_specs=[VMEM] * 12,
        out_specs=[VMEM] * 4,
        out_shape=[made(*PLAIN)] * 4,
        scratch_shapes=[small(*PLAIN)]
        + [small(*RIM)] * 4
        + [small(*CARRY), small(2, GROUP, COLS)],
        cost_estimate=cost(4),
        compiler_params=limit(12),
        name="settle",
    )(const, *steps, inverse, weight, face_e, face_n, ghost, fix, rhs)
    return pl.pallas_call(
        finish,
        in_specs=[VMEM] * 12,
        out_specs=[ANYWHERE] * 4,
        out_shape=[made(*PLAIN)] * 4,
        scratch_shapes=[small(4, PAYLOAD, LANES)]
        + [small(*RIM)] * 3
        + [small(LANES, LANES)] * 2
        + [small(*PLAIN)] * 4
        + [pltpu.SemaphoreType.DMA((BLOCKS, 4))],
        cost_estimate=cost(3),
        compiler_params=limit(12),
        name="finish",
    )(const, *steps, inverse, weight, rim_face, c_sent, d_sent, c_got, d_got)


def on_device(heat, salt, east, north, marine, mixing, spacing, spin, hinge, partner):
    cells = (heat, salt, east, north, marine, mixing)
    edges = [pltpu.VMEM((2, x.shape[0], TILE, COLS), x.dtype) for x in cells]
    anchor, a_sent, b_sent, own, const, spins, *cells = pl.pallas_call(
        pack_rows,
        in_specs=[ANYWHERE] * 10,
        out_specs=[SMEM] + [VMEM] * 11,
        out_shape=[pltpu.SMEM((1,), jnp.int32)]
        + [made(PAYLOAD, COLS)] * 2
        + [made(2, PAYLOAD, COLS), made(OPEN_NORTH + TILE, COLS), made(LANES, LANES)]
        + [jax.ShapeDtypeStruct(x.shape, x.dtype) for x in cells],
        scratch_shapes=[
            pltpu.SMEM((1,), jnp.int32),
            pltpu.SMEM((COLS,), jnp.int32),
            pltpu.SMEM((LEVELS,), jnp.float32),
            small(1, ROWS),
            *edges,
            pltpu.SemaphoreType.DMA((22,)),
        ],
        cost_estimate=cost(2),
        compiler_params=limit(8),
        name="pack_rows",
    )(hinge, *[pltpu.with_memory_space_constraint(x, pltpu.HBM) for x in (partner, spacing, spin.reshape(1, -1), *cells)])
    branches = [functools.partial(inner_beside_rows, k) for k in range(lax.axis_size("lon"))]
    got = lax.switch(anchor[0], branches, a_sent, b_sent, own, const, spins, cells)
    return columns_and_finish(*got, const)


def solution(mesh):
    cells = P(None, "lat", "lon")
    return jax.shard_map(
        on_device,
        mesh=mesh,
        in_specs=(cells,) * 6 + (P(), P("lat"), P(), P("lon")),
        out_specs=(cells,) * 4,
        check_vma=False,
    )
```

```python
import functools

import jax
import jax.numpy as jnp
from jax import lax
from jax.experimental import pallas as pl
from jax.experimental.pallas import tpu as pltpu
from jax.sharding import PartitionSpec as P

LEVELS = 10
ROWS = 64
COLS = 256
TILE = 8
BLOCKS = ROWS // TILE
LANES = 128
GROUP = 16
HEAT, SALT, EAST, NORTH, WET, PART, MIX = 0, 10, 20, 30, 40, 50, 60
PAYLOAD = 72
SOUTH_LANE, NORTH_LANE = 64, 65
GRAIN = 0.06
OPEN_NORTH = 16
DRY = 1.0e30


def iota(shape, dim):
    return lax.broadcasted_iota(jnp.int32, shape, dim)


def weights(both, speeds):
    speed = 0.1 * speeds
    here = jnp.maximum(speed, 0.0) + GRAIN
    return both * here, both * (speed - here)


def east_of(x):
    return pltpu.roll(x, x.shape[1] - 1, 1)


def west_of(x):
    return pltpu.roll(x, 1, 1)


def north_of(x, block_above, sub):
    return pltpu.roll(jnp.where(sub == 0, block_above, x), TILE - 1, 0)


def south_of(x, block_below, sub):
    return pltpu.roll(jnp.where(sub == TILE - 1, block_below, x), 1, 0)


def mix_down(heat, salt):
    return 0.8 * salt - 0.2 * heat


def tile_rows(block):
    return pl.ds(pl.multiple_of(block * TILE, TILE), TILE)


def pack_rows(
    hinge_hbm, partner_hbm, thick_hbm, spin_hbm,
    heat_hbm, salt_hbm, east_hbm, north_hbm, wet_hbm, mix_hbm,
    anchor_ref, a_ref, b_ref, own_ref, const_ref, spins_ref,
    heat_in, salt_in, east_in, north_in, wet_in, mix_in,
    hinge_ref, partner_ref, thick_ref, spin_ref,
    heat_e, salt_e, east_e, north_e, wet_e, mix_e, sems,
):
    sources = (heat_hbm, salt_hbm, east_hbm, north_hbm, wet_hbm, mix_hbm)
    edges = (heat_e, salt_e, east_e, north_e, wet_e, mix_e)
    pairs = [(hinge_hbm, hinge_ref), (partner_hbm, partner_ref), (thick_hbm, thick_ref), (spin_hbm, spin_ref)]
    for side, first in ((0, 0), (1, ROWS - TILE)):
        pairs += [(src.at[:, pl.ds(first, TILE)], dst.at[side]) for src, dst in zip(sources, edges)]
    early = len(pairs)
    pairs += zip(sources, (heat_in, salt_in, east_in, north_in, wet_in, mix_in))
    copies = [pltpu.make_async_copy(src, dst, sems.at[i]) for i, (src, dst) in enumerate(pairs)]
    for copy in copies:
        copy.start()
    for copy in copies[:early]:
        copy.wait()
    lon = lax.axis_size("lon")
    anchor_ref[0] = (partner_ref[0] + 1 + COLS * lax.axis_index("lon")) // COLS % lon
    for level in range(LEVELS):
        const_ref[level : level + 1] = jnp.full((1, COLS), thick_ref[level], jnp.float32)
    spins_ref[0:1] = jnp.zeros((1, LANES), jnp.float32)
    spins_ref[0:1, :ROWS] = 0.2 * spin_ref[...]
    spins_ref[...] = jnp.transpose(jnp.broadcast_to(spins_ref[0:1], (LANES, LANES)))
    bottom, top = ([ref.at[side] for ref in edges] for side in range(2))
    lat = lax.axis_index("lat")
    at_top = lat == lax.axis_size("lat") - 1
    even = lat % 2 == 0
    hinged = jnp.logical_and(at_top, hinge_ref[0] == 1)
    const_ref[OPEN_NORTH : OPEN_NORTH + 1] = jnp.full((1, COLS), jnp.where(hinged, 0.0, 1.0), jnp.float32)
    inner = (iota((TILE, COLS), 1) < COLS - 1).astype(jnp.float32)
    sub = iota((TILE, COLS), 0)
    for level in range(LEVELS):
        sides = []
        for heat_ref, salt_ref, east_ref, north_ref, wet_ref, mix_ref in (bottom, top):
            heat, salt = heat_ref[level], salt_ref[level]
            east, north = east_ref[level], north_ref[level]
            wet = wet_ref[level].astype(jnp.float32)
            mixed = mix_down(heat, salt)
            here, there = weights(wet * inner * east_of(wet), east + east_of(east))
            flux_e = here * mixed + there * east_of(mixed)
            above = lambda x: pltpu.roll(x, TILE - 1, 0)
            here, there = weights(wet * above(wet), north + above(north))
            flux_n = here * mixed + there * above(mixed)
            part = mixed - (flux_e - west_of(flux_e))
            sides.append((heat, salt, east, north, wet, part, mix_ref[min(level, LEVELS - 2)], flux_n))
        *low, flux_n = sides[0]
        low[5] = low[5] - flux_n
        low = [x[:1] for x in low]
        *high, flux_n = sides[1]
        flux_s = pltpu.roll(flux_n, 1, 0)
        high[5] = high[5] + flux_s - jnp.where(sub == TILE - 1, 0.0, flux_n)
        last = [x[TILE - 1 :] for x in high]
        high = [jnp.where(hinged, x[TILE - 2 : TILE - 1], end) for x, end in zip(high, last)]
        for start, one, other, end in zip((HEAT, SALT, EAST, NORTH, WET, PART, MIX), low, high, last):
            if start == MIX and level == LEVELS - 1:
                continue
            row = slice(start + level, start + level + 1)
            a_ref[row] = jnp.where(even, other, one)
            b_ref[row] = jnp.where(even, one, other)
            own_ref[0, row] = one
            own_ref[1, row] = end
    for ref in (a_ref, b_ref):
        ref[MIX + LEVELS - 1 :] = jnp.zeros((PAYLOAD - MIX - LEVELS + 1, COLS), jnp.float32)

    @pl.when(at_top)
    def _():
        back = LANES - 1 - iota((TILE, LANES), 1)
        for row in range(0, PAYLOAD, TILE):
            place = row + iota((TILE, LANES), 0)
            sign = jnp.where(jnp.logical_and(place >= EAST, place < WET), -1.0, 1.0)
            left = b_ref[row : row + TILE, :LANES]
            right = b_ref[row : row + TILE, LANES:]
            flip = lambda x: sign * jnp.take_along_axis(x, back, axis=1, mode="promise_in_bounds")
            b_ref[row : row + TILE, :LANES] = flip(right)
            b_ref[row : row + TILE, LANES:] = flip(left)

    for copy in copies[early:]:
        copy.wait()


def factor(thick, mix, wet):
    inverse, weight, ratio = [], [], []
    for level in range(LEVELS):
        diagonal = thick[level]
        if level < LEVELS - 1:
            weight.append((0.2 * mix[level]) * (wet[level] * wet[level + 1]))
            diagonal = diagonal + weight[level]
        if level > 0:
            diagonal = diagonal + weight[level - 1] * (1.0 - ratio[level - 1])
        inverse.append(1.0 / diagonal)
        if level < LEVELS - 1:
            ratio.append(weight[level] * inverse[level])
    return inverse, weight, ratio


def solve(thick, inverse, weight, ratio, right):
    x = []
    for level in range(LEVELS):
        now = thick[level] * right[level]
        if level > 0:
            now = now + weight[level - 1] * x[level - 1]
        x.append(now * inverse[level])
    for level in reversed(range(LEVELS - 1)):
        x[level] = x[level] + ratio[level] * x[level + 1]
    return x


def pressures(thick, density):
    above, out = None, []
    for level in range(LEVELS):
        layer = (0.1 * thick[level]) * density[level]
        out.append(0.5 * layer if above is None else above + 0.5 * layer)
        above = layer if above is None else above + layer
    return out


def thicknesses(const_ref, width):
    return [const_ref[level : level + 1, :width] for level in range(LEVELS)]


def inner_steps(
    const_ref, spins, heat_ref, salt_ref, east_ref, north_ref, wet_ref, mix_ref,
    heat_out, salt_out, east_out, north_out, inv_out, weight_out, face_e_out, face_n_out, rim_out, rim_face_out,
    heat_f, salt_f, east_f, north_f, rim, rim_face,
):
    thick = thicknesses(const_ref, COLS)
    inner = (iota((TILE, COLS), 1) < COLS - 1).astype(jnp.float32)
    sub = iota((TILE, COLS), 0)
    lane = iota((TILE, LANES), 1)
    for ref in (heat_f, salt_f, east_f, north_f):
        ref[...] = jnp.zeros(ref.shape, jnp.float32)

    def both_ends(x, east_lane):
        west = jnp.where(lane == 0, x[:, :LANES], 0.0)
        return jnp.where(lane == east_lane, x[:, LANES:], west)

    def step(block, _):
        rows = tile_rows(block)
        above = tile_rows(jnp.minimum(block + 1, BLOCKS - 1))
        shut = jnp.logical_and(sub == TILE - 1, block == BLOCKS - 1)
        spin = spins[rows]
        spin = jnp.concatenate([spin, spin], axis=1)
        ends = jnp.zeros((TILE, LANES), jnp.float32)
        end_faces = ends
        all_wet, all_mix, all_flows, changes = [], [], [], []
        stack = lambda ref: ref[:, rows].reshape(LEVELS * TILE, COLS)
        heat_all, salt_all, north_all = (east_of(stack(ref)) for ref in (heat_ref, salt_ref, north_ref))
        coded_all = jnp.where(stack(wet_ref) > 0, stack(east_ref), DRY)
        coded_east = east_of(coded_all)
        for level in range(LEVELS):
            mine = slice(level * TILE, level * TILE + TILE)
            pick = lambda ref: (ref[level, rows], north_of(ref[level, rows], ref[level, above], sub))
            heat, heat_n = pick(heat_ref)
            salt, salt_n = pick(salt_ref)
            east, east_n = pick(east_ref)
            north, north_n = pick(north_ref)
            wet, wet_n = (x.astype(jnp.float32) for x in pick(wet_ref))
            all_wet.append(wet)
            both = jnp.where(shut, 0.0, wet * wet_n)
            face_n_out[level, rows] = 0.1 * both
            here, there = weights(both, north + north_n)
            spread = GRAIN * both
            flows = [
                here * heat + there * heat_n,
                here * salt + there * salt_n,
                spread * (east_n - east),
                spread * (north_n - north),
            ]
            change = []
            for ref, flow in zip((heat_f, salt_f, east_f, north_f), flows):
                change.append(flow - south_of(flow, ref[level], sub))
                ref[level] = flow
            coded, coded_e = coded_all[mine], coded_east[mine]
            both = jnp.where(coded_e < 0.5 * DRY, wet * inner, 0.0)
            face = 0.1 * both
            face_e_out[level, rows] = face
            place = 4 * level
            end_faces = end_faces + pltpu.roll(both_ends(face, LANES - 2), place + 2, 1)
            here, there = weights(both, coded_e + east)
            spread = GRAIN * both
            flows = [
                here * heat + there * heat_all[mine],
                here * salt + there * salt_all[mine],
                spread * (coded_e - east),
                spread * (north_all[mine] - north),
            ]
            changes.append([n + flow for n, flow in zip(change, flows)])
            all_flows.append(flows)
        all_flows = [west_of(jnp.concatenate(one, axis=0)) for one in zip(*all_flows)]
        for level in range(LEVELS):
            mine = slice(level * TILE, level * TILE + TILE)
            change = [n - flow[mine] for n, flow in zip(changes[level], all_flows)]
            heat, salt = heat_ref[level, rows], salt_ref[level, rows]
            east, north = east_ref[level, rows], north_ref[level, rows]
            wet, coded = all_wet[level], coded_all[mine]
            new_heat = heat - change[0]
            new_salt = salt - change[1]
            heat_out[level, rows] = new_heat
            salt_out[level, rows] = new_salt
            turn = wet * spin
            east_out[level, rows] = east + (turn * north + change[2])
            north_out[level, rows] = north + (change[3] - turn * east)
            fields = [heat, salt, coded, north, mix_down(new_heat, new_salt)]
            if level < LEVELS - 1:
                all_mix.append(mix_ref[level, rows])
                fields.append(all_mix[level])
            for which, x in enumerate(fields):
                place = 2 * (which * LEVELS + level)
                ends = ends + pltpu.roll(both_ends(x, LANES - 1), place + 1, 1)
        rim[rows] = ends
        rim_face[rows] = end_faces
        inverse, weight, _ = factor(thick, all_mix, all_wet)
        for level in range(LEVELS):
            inv_out[level, rows] = inverse[level]
            if level < LEVELS - 1:
                weight_out[level, rows] = weight[level]
        return 0

    lax.fori_loop(0, BLOCKS, step, 0)
    wide = iota((LANES, LANES), 1)
    rim[...] = jnp.where(wide < ROWS, jnp.transpose(rim[...]), 0.0)
    rim_face[...] = jnp.where(wide < ROWS, jnp.transpose(rim_face[...]), 0.0)
    for side, first in ((0, 1), (1, 0)):
        rim_face_out[side, :LEVELS] = rim_face[pl.ds(2 * first, LEVELS, 4)]
        ends = rim[pl.ds(first, ROWS, 2)]
        coded = ends[EAST : EAST + LEVELS]
        rim_out[side, HEAT:EAST] = ends[HEAT:EAST]
        rim_out[side, EAST : EAST + LEVELS] = jnp.where(coded < DRY, coded, 0.0)
        rim_out[side, NORTH : NORTH + LEVELS] = ends[30:40]
        rim_out[side, WET : WET + LEVELS] = jnp.where(coded < DRY, 1.0, 0.0)
        rim_out[side, PART : PART + 2 * LEVELS] = ends[40:60]
        rim_out[side, PART + 2 * LEVELS :] = jnp.zeros((PAYLOAD - PART - 2 * LEVELS, LANES), jnp.float32)


def from_lat(a_ref, b_ref):
    even = lax.axis_index("lat") % 2 == 0
    a, b = a_ref[...], b_ref[...]
    return jnp.where(even, b, a), jnp.where(even, a, b)


def row_faces(const_ref, a_ref, b_ref, own_ref, rim_ref, fix_out, rhs_out, c_out, d_out, ghost):
    open_north = const_ref[OPEN_NORTH : OPEN_NORTH + 1]
    ghost[0], ghost[1] = from_lat(a_ref, b_ref)
    mixed_flux = []
    for side in range(2):
        mine = lambda start: own_ref[side, start : start + LEVELS]
        other = lambda start: ghost[side, start : start + LEVELS]
        low, high = (other, mine) if side == 0 else (mine, other)
        sign = 1.0 if side == 0 else -1.0
        both = low(WET) * high(WET)
        here, there = weights(both, low(NORTH) + high(NORTH))
        spread = -sign * GRAIN * both
        heat_n = here * low(HEAT) + there * high(HEAT)
        salt_n = here * low(SALT) + there * high(SALT)
        changes = (
            sign * heat_n,
            sign * salt_n,
            spread * (high(EAST) - low(EAST)),
            spread * (high(NORTH) - low(NORTH)),
            0.1 * both,
        )
        for which, change in enumerate(changes):
            base = (side * len(changes) + which) * GROUP
            fix_out[base : base + LEVELS] = change
        flux = mix_down(heat_n, salt_n)
        mixed_flux.append(flux)
        change = -flux if side == 0 else open_north * flux
        rhs_out[side * GROUP : side * GROUP + LEVELS] = other(PART) + change
    lane = iota((LEVELS, LANES), 1)
    wide = iota((PAYLOAD, LANES), 1)
    sides = []
    for side, column in ((0, 0), (1, COLS - 1)):
        ends = rim_ref[side]
        for place, which in ((SOUTH_LANE, 0), (NORTH_LANE, 1)):
            ends = jnp.where(wide == place, ghost[which, :, column : column + 1], ends)
        part = rim_ref[side, PART : PART + LEVELS]
        part = part + jnp.where(lane == 0, mixed_flux[0][:, column : column + 1], 0.0)
        part = part - jnp.where(lane == ROWS - 1, mixed_flux[1][:, column : column + 1], 0.0)
        sides.append((ends, part))
    even = lax.axis_index("lon") % 2 == 0
    c_out[...] = jnp.where(even, sides[1][0], sides[0][0])
    d_out[...] = jnp.where(even, sides[0][0], sides[1][0])
    c_out[PART : PART + LEVELS] = jnp.where(even, sides[1][1], sides[0][1])
    d_out[PART : PART + LEVELS] = jnp.where(even, sides[0][1], sides[1][1])


def bands_at(inv_ref, weight_ref, rows):
    inverse = [inv_ref[level, rows] for level in range(LEVELS)]
    weight = [weight_ref[level, rows] for level in range(LEVELS - 1)]
    return inverse, weight, [w * inv for w, inv in zip(weight, inverse)]


def settle(
    const_ref, heat_ref, salt_ref, east_ref, north_ref, inv_ref, weight_ref, face_e_ref, face_n_ref,
    ghost, fix_ref, rhs_ref,
    heat_out, salt_out, east_out, north_out,
    press_x, rim_rhs, rim_mix, rim_wet, rim_press, north_f, outer_p,
):
    for level in range(LEVELS):
        for slot in range(TILE):
            side, half = slot // 2 % 2, slot % 2 * LANES
            row = side * GROUP + level
            rim_rhs[level, slot : slot + 1] = rhs_ref[row : row + 1, half : half + LANES]
            for ref, start in ((rim_mix, MIX), (rim_wet, WET)):
                row = start + level
                ref[level, slot : slot + 1] = ghost[side, row : row + 1, half : half + LANES]
    listed = lambda ref: [ref[level] for level in range(LEVELS)]
    thin = thicknesses(const_ref, LANES)
    rim_density = solve(thin, *(bands := factor(thin, listed(rim_mix), listed(rim_wet))), listed(rim_rhs))
    for level, value in enumerate(pressures(thin, rim_density)):
        rim_press[level] = value
        for slot in range(4):
            half = slot % 2 * LANES
            outer_p[slot // 2, level : level + 1, half : half + LANES] = rim_press[level, slot : slot + 1]

    for level in range(LEVELS):
        for side, row in ((0, 0), (1, ROWS - 1)):
            for which, (src, out) in enumerate(
                ((heat_ref, heat_out), (salt_ref, salt_out), (east_ref, east_out), (north_ref, north_out))
            ):
                place = (side * 5 + which) * GROUP + level
                out[level, row : row + 1] = src[level, row : row + 1] + fix_ref[place : place + 1]
    thick = thicknesses(const_ref, COLS)
    sub = iota((TILE, COLS), 0)

    def tracers(block, _):
        rows = tile_rows(block)
        bands = bands_at(inv_ref, weight_ref, rows)
        first = jnp.logical_and(block == 0, sub == 0)
        last = jnp.logical_and(block == BLOCKS - 1, sub == TILE - 1)
        fixed = jnp.logical_or(first, last)
        take = lambda src, out: [jnp.where(fixed, out[level, rows], src[level, rows]) for level in range(LEVELS)]
        heat = solve(thick, *bands, take(heat_ref, heat_out))
        salt = solve(thick, *bands, take(salt_ref, salt_out))
        density = [mix_down(h, s) for h, s in zip(heat, salt)]
        for level, value in enumerate(pressures(thick, density)):
            heat_out[level, rows] = heat[level]
            salt_out[level, rows] = salt[level]
            press_x[level, rows] = value
        return 0

    lax.fori_loop(0, BLOCKS, tracers, 0)
    for level in range(LEVELS):
        north_f[level] = jnp.zeros((TILE, COLS), jnp.float32)
        for side, row in ((0, 0), (1, ROWS - 1)):
            place = (side * 5 + 4) * GROUP + level
            outer = outer_p[side, level : level + 1]
            slope = fix_ref[place : place + 1] * (press_x[level, row : row + 1] - outer)
            north_out[level, row : row + 1] += slope if side == 1 else -slope

    def flow(block, _):
        rows = tile_rows(block)
        above = tile_rows(jnp.minimum(block + 1, BLOCKS - 1))
        first = jnp.logical_and(block == 0, sub == 0)
        last = jnp.logical_and(block == BLOCKS - 1, sub == TILE - 1)
        fixed = jnp.logical_or(first, last)
        for level in range(LEVELS):
            press = press_x[level, rows]
            press_n = north_of(press, press_x[level, above], sub)
            slope_n = face_n_ref[level, rows] * (press_n - press)
            slope_s = south_of(slope_n, north_f[level], sub)
            north_f[level] = slope_n
            slope_e = face_e_ref[level, rows] * (east_of(press) - press)
            east = jnp.where(fixed, east_out[level, rows], east_ref[level, rows])
            north = jnp.where(fixed, north_out[level, rows], north_ref[level, rows])
            east_out[level, rows] = east - (slope_e + west_of(slope_e))
            north_out[level, rows] = north - (slope_n + slope_s)
        return 0

    lax.fori_loop(0, BLOCKS, flow, 0)


def row_shifts(x, lane):
    after = jnp.where(lane == ROWS, pltpu.roll(x, LANES - 1, 1), x)
    before = jnp.where(lane == LANES - 1, pltpu.roll(x, LANES - 1 - SOUTH_LANE, 1), x)
    return pltpu.roll(after, LANES - 1, 1), pltpu.roll(before, 1, 1)


def finish(
    const_ref, heat_ref, salt_ref, east_ref, north_ref, inv_ref, weight_ref, rim_face_ref,
    d_own_ref, c_own_ref, d_ref, c_ref,
    heat_out, salt_out, east_out, north_out,
    rims, rim_rhs, rim_mix, rim_wet, rim_rows, fixes, heat_x, salt_x, east_x, north_x, sems,
):
    even = lax.axis_index("lon") % 2 == 0
    rims[0] = jnp.where(even, d_own_ref[...], c_own_ref[...])
    rims[1] = jnp.where(even, d_ref[...], c_ref[...])
    rims[2] = jnp.where(even, c_own_ref[...], d_own_ref[...])
    rims[3] = jnp.where(even, c_ref[...], d_ref[...])
    span = lambda which, start: rims[which, start : start + LEVELS]
    slots = lambda slot: slice(GROUP * slot, GROUP * slot + LEVELS)
    lane = iota((LEVELS, LANES), 1)
    sides = ((1, 0), (2, 3))
    for side, (left, right) in enumerate(sides):
        both = span(left, WET) * span(right, WET)
        here, there = weights(both, span(left, EAST) + span(right, EAST))
        heat_e = here * span(left, HEAT) + there * span(right, HEAT)
        salt_e = here * span(left, SALT) + there * span(right, SALT)
        own = 1.0 if side == 0 else -1.0
        rim_rows[slots(2 * side)] = own * heat_e
        rim_rows[slots(2 * side + 1)] = own * salt_e
        rim_rows[slots(4 + side)] = span(2 * side + 1, PART) - own * mix_down(heat_e, salt_e)
        rim_rows[slots(6 + side)] = span(2 * side, PART)
    source = (0, 0, 2, 2, 1, 3, 0, 2)
    for level in range(LEVELS):
        for slot in range(TILE):
            rim_rhs[level, slot : slot + 1] = rim_rows[GROUP * slot + level : GROUP * slot + level + 1]
            for ref, start in ((rim_mix, MIX), (rim_wet, WET)):
                ref[level, slot : slot + 1] = rims[source[slot], start + level : start + level + 1]
    listed = lambda ref: [ref[level] for level in range(LEVELS)]
    thin = thicknesses(const_ref, LANES)
    solved = solve(thin, *factor(thin, listed(rim_mix), listed(rim_wet)), listed(rim_rhs))
    for level, value in enumerate(solved):
        rim_rhs[level] = value
        for slot in range(TILE):
            rim_rows[GROUP * slot + level : GROUP * slot + level + 1] = rim_rhs[level, slot : slot + 1]

    def pressed(density):
        out = pressures(thin, [density[level : level + 1] for level in range(LEVELS)])
        return jnp.concatenate(out, axis=0)

    for side, (left, right) in enumerate(sides):
        heat, salt = rim_rows[slots(2 * side)], rim_rows[slots(2 * side + 1)]
        change = pressed(mix_down(heat, salt))
        mine = pressed(rim_rows[slots(6 + side)]) + change
        other = pressed(rim_rows[slots(4 + side)])
        low, high = (other, mine) if side == 0 else (mine, other)
        both = span(left, WET) * span(right, WET)
        own = -1.0 if side == 0 else 1.0
        slope = 0.1 * both * (high - low)
        inner = rim_face_ref[side, :LEVELS] * change
        inner = inner if side == 0 else -inner
        wet = span(2 * side, WET)
        wet_n, wet_s = row_shifts(wet, lane)
        change_n, change_s = row_shifts(change, lane)
        pull = 0.1 * (wet * wet_n * (change_n - change) + wet * wet_s * (change - change_s))
        east = own * GRAIN * both * (span(right, EAST) - span(left, EAST)) - slope + inner
        north = own * GRAIN * both * (span(right, NORTH) - span(left, NORTH)) - pull
        west_side = 1 - side
        fixes[pl.ds(1 + west_side, LEVELS, 4)] = east
        fixes[pl.ds(3 * west_side, LEVELS, 4)] = inner
        for which, value in enumerate((heat, salt, north)):
            fixes[pl.ds(40 + 20 * which + west_side, LEVELS, 2)] = value
    fixes[...] = jnp.transpose(fixes[...])
    thick = thicknesses(const_ref, COLS)
    lanes = iota((TILE, LANES), 1)

    def fix(corner, place, reach):
        turned = pltpu.roll(corner, LANES - place, 1)
        west = jnp.where(lanes < reach, turned, 0.0)
        east = jnp.where(lanes >= LANES - reach, turned, 0.0)
        return jnp.concatenate([west, east], axis=1)

    def leave(block):
        rows = tile_rows(block)
        pairs = ((heat_x, heat_out), (salt_x, salt_out), (east_x, east_out), (north_x, north_out))
        return [
            pltpu.make_async_copy(src.at[:, rows], dst.at[:, rows], sems.at[block, i])
            for i, (src, dst) in enumerate(pairs)
        ]

    def flow(block, _):
        rows = tile_rows(block)
        corner = fixes[rows]
        new_east, new_north = [], []
        for level in range(LEVELS):
            heat_x[level, rows] = heat_ref[level, rows] + fix(corner, 41 + 2 * level, 1)
            salt_x[level, rows] = salt_ref[level, rows] + fix(corner, 61 + 2 * level, 1)
            new_east.append(east_ref[level, rows] + fix(corner, 4 * level + 2, 2))
            new_north.append(north_ref[level, rows] + fix(corner, 81 + 2 * level, 1))
        bands = bands_at(inv_ref, weight_ref, rows)
        for out, right in ((east_x, new_east), (north_x, new_north)):
            for level, value in enumerate(solve(thick, *bands, right)):
                out[level, rows] = value
        for copy in leave(block):
            copy.start()
        return 0

    lax.fori_loop(0, BLOCKS, flow, 0)
    for block in range(BLOCKS):
        for copy in leave(block):
            copy.wait()


def swap_in_pairs(x, axis, first):
    count = lax.axis_size(axis)
    return lax.ppermute(x, axis, [(i, (((i - first) ^ 1) + first) % count) for i in range(count)])


def swap_with_fold(x, anchor):
    lon, lat = lax.axis_size("lon"), lax.axis_size("lat")
    pairs = []
    for i in range(lon):
        for j in range(1, lat - 1):
            pairs.append((i * lat + j, i * lat + ((j - 1) ^ 1) + 1))
        pairs.append((i * lat + lat - 1, (anchor - 1 - i) % lon * lat + lat - 1))
    return lax.ppermute(x, ("lon", "lat"), pairs)


SMEM = pl.BlockSpec(memory_space=pltpu.SMEM)
VMEM = pl.BlockSpec(memory_space=pltpu.VMEM)
ANYWHERE = pl.BlockSpec(memory_space=pl.ANY)


def small(*shape):
    return pltpu.VMEM(shape, jnp.float32)


def made(*shape):
    return jax.ShapeDtypeStruct(shape, jnp.float32)


PLAIN = (LEVELS, ROWS, COLS)
LESS = (LEVELS - 1, ROWS, COLS)
CARRY = (LEVELS, TILE, COLS)
RIM = (LEVELS, TILE, LANES)


def limit(mib):
    return pltpu.CompilerParams(vmem_limit_bytes=mib * 2**20)


def cost(micros):
    return pl.CostEstimate(flops=0, bytes_accessed=int(micros * 3.5e6), transcendentals=0)


def inner_beside_rows(anchor, a_sent, b_sent, own, const, spins, cells):
    a_got = swap_in_pairs(a_sent, "lat", 0)
    b_got = swap_with_fold(b_sent, anchor)
    *steps, rim, rim_face = pl.pallas_call(
        inner_steps,
        in_specs=[VMEM] * 8,
        out_specs=[VMEM] * 10,
        out_shape=[made(*PLAIN)] * 5 + [made(*LESS)] + [made(*PLAIN)] * 2
        + [made(2, PAYLOAD, LANES), made(2, GROUP, LANES)],
        scratch_shapes=[small(*CARRY)] * 4 + [small(LANES, LANES)] * 2,
        cost_estimate=cost(5),
        compiler_params=limit(16),
        name="inner_steps",
    )(const, spins, *cells)
    faces = pl.pallas_call(
        row_faces,
        in_specs=[VMEM] * 5,
        out_specs=[VMEM] * 5,
        out_shape=[made(10 * GROUP, COLS), made(2 * GROUP, COLS)] + [made(PAYLOAD, LANES)] * 2
        + [made(2, PAYLOAD, COLS)],
        cost_estimate=cost(0.5),
        compiler_params=limit(4),
        name="row_faces",
    )(const, a_got, b_got, own, rim)
    return faces, steps, rim_face


def columns_and_finish(faces, steps, rim_face, const):
    fix, rhs, c_sent, d_sent, ghost = faces
    c_got = swap_in_pairs(c_sent, "lon", 0)
    d_got = swap_in_pairs(d_sent, "lon", 1)
    *steps, inverse, weight, face_e, face_n = steps
    steps = pl.pallas_call(
        settle,
        in_specs=[VMEM] * 12,
        out_specs=[VMEM] * 4,
        out_shape=[made(*PLAIN)] * 4,
        scratch_shapes=[small(*PLAIN)]
        + [small(*RIM)] * 4
        + [small(*CARRY), small(2, GROUP, COLS)],
        cost_estimate=cost(4),
        compiler_params=limit(12),
        name="settle",
    )(const, *steps, inverse, weight, face_e, face_n, ghost, fix, rhs)
    return pl.pallas_call(
        finish,
        in_specs=[VMEM] * 12,
        out_specs=[ANYWHERE] * 4,
        out_shape=[made(*PLAIN)] * 4,
        scratch_shapes=[small(4, PAYLOAD, LANES)]
        + [small(*RIM)] * 3
        + [small(LANES, LANES)] * 2
        + [small(*PLAIN)] * 4
        + [pltpu.SemaphoreType.DMA((BLOCKS, 4))],
        cost_estimate=cost(3),
        compiler_params=limit(12),
        name="finish",
    )(const, *steps, inverse, weight, rim_face, d_sent, c_sent, d_got, c_got)


def on_device(heat, salt, east, north, marine, mixing, spacing, spin, hinge, partner):
    cells = (heat, salt, east, north, marine, mixing)
    edges = [pltpu.VMEM((2, x.shape[0], TILE, COLS), x.dtype) for x in cells]
    anchor, a_sent, b_sent, own, const, spins, *cells = pl.pallas_call(
        pack_rows,
        in_specs=[ANYWHERE] * 10,
        out_specs=[SMEM] + [VMEM] * 11,
        out_shape=[pltpu.SMEM((1,), jnp.int32)]
        + [made(PAYLOAD, COLS)] * 2
        + [made(2, PAYLOAD, COLS), made(OPEN_NORTH + TILE, COLS), made(LANES, LANES)]
        + [jax.ShapeDtypeStruct(x.shape, x.dtype) for x in cells],
        scratch_shapes=[
            pltpu.SMEM((1,), jnp.int32),
            pltpu.SMEM((COLS,), jnp.int32),
            pltpu.SMEM((LEVELS,), jnp.float32),
            small(1, ROWS),
            *edges,
            pltpu.SemaphoreType.DMA((22,)),
        ],
        cost_estimate=cost(2),
        compiler_params=limit(8),
        name="pack_rows",
    )(hinge, *[pltpu.with_memory_space_constraint(x, pltpu.HBM) for x in (partner, spacing, spin.reshape(1, -1), *cells)])
    branches = [functools.partial(inner_beside_rows, k) for k in range(lax.axis_size("lon"))]
    got = lax.switch(anchor[0], branches, a_sent, b_sent, own, const, spins, cells)
    return columns_and_finish(*got, const)


def solution(mesh):
    cells = P(None, "lat", "lon")
    return jax.shard_map(
        on_device,
        mesh=mesh,
        in_specs=(cells,) * 6 + (P(), P("lat"), P(), P("lon")),
        out_specs=(cells,) * 4,
        check_vma=False,
    )
```

```python
import functools

import jax
import jax.numpy as jnp
from jax import lax
from jax.experimental import pallas as pl
from jax.experimental.pallas import tpu as pltpu
from jax.sharding import PartitionSpec as P

LEVELS = 10
ROWS = 64
COLS = 256
TILE = 8
BLOCKS = ROWS // TILE
LANES = 128
GROUP = 16
HEAT, SALT, EAST, NORTH, WET, PART, MIX = 0, 10, 20, 30, 40, 50, 60
PAYLOAD = 72
SOUTH_LANE, NORTH_LANE = 64, 65
GRAIN = 0.06
OPEN_NORTH = 16
DRY = 1.0e30


def iota(shape, dim):
    return lax.broadcasted_iota(jnp.int32, shape, dim)


def weights(both, speeds):
    speed = 0.1 * speeds
    here = jnp.maximum(speed, 0.0) + GRAIN
    return both * here, both * (speed - here)


def east_of(x):
    return pltpu.roll(x, x.shape[1] - 1, 1)


def west_of(x):
    return pltpu.roll(x, 1, 1)


def north_of(x, block_above, sub):
    return pltpu.roll(jnp.where(sub == 0, block_above, x), TILE - 1, 0)


def south_of(x, block_below, sub):
    return pltpu.roll(jnp.where(sub == TILE - 1, block_below, x), 1, 0)


def mix_down(heat, salt):
    return 0.8 * salt - 0.2 * heat


def tile_rows(block):
    return pl.ds(pl.multiple_of(block * TILE, TILE), TILE)


def pack_rows(
    hinge_hbm, partner_hbm, thick_hbm, spin_hbm,
    heat_hbm, salt_hbm, east_hbm, north_hbm, wet_hbm, mix_hbm,
    anchor_ref, a_ref, b_ref, own_ref, const_ref, spins_ref,
    heat_in, salt_in, east_in, north_in, wet_in, mix_in,
    hinge_ref, partner_ref, thick_ref, spin_ref,
    heat_e, salt_e, east_e, north_e, wet_e, mix_e, sems,
):
    sources = (heat_hbm, salt_hbm, east_hbm, north_hbm, wet_hbm, mix_hbm)
    edges = (heat_e, salt_e, east_e, north_e, wet_e, mix_e)
    pairs = [(hinge_hbm, hinge_ref), (partner_hbm, partner_ref), (thick_hbm, thick_ref), (spin_hbm, spin_ref)]
    for side, first in ((0, 0), (1, ROWS - TILE)):
        pairs += [(src.at[:, pl.ds(first, TILE)], dst.at[side]) for src, dst in zip(sources, edges)]
    early = len(pairs)
    pairs += zip(sources, (heat_in, salt_in, east_in, north_in, wet_in, mix_in))
    copies = [pltpu.make_async_copy(src, dst, sems.at[i]) for i, (src, dst) in enumerate(pairs)]
    for copy in copies:
        copy.start()
    for copy in copies[:early]:
        copy.wait()
    lon = lax.axis_size("lon")
    anchor_ref[0] = (partner_ref[0] + 1 + COLS * lax.axis_index("lon")) // COLS % lon
    for level in range(LEVELS):
        const_ref[level : level + 1] = jnp.full((1, COLS), thick_ref[level], jnp.float32)
    spins_ref[0:1] = jnp.zeros((1, LANES), jnp.float32)
    spins_ref[0:1, :ROWS] = 0.2 * spin_ref[...]
    spins_ref[...] = jnp.transpose(jnp.broadcast_to(spins_ref[0:1], (LANES, LANES)))
    bottom, top = ([ref.at[side] for ref in edges] for side in range(2))
    lat = lax.axis_index("lat")
    at_top = lat == lax.axis_size("lat") - 1
    even = lat % 2 == 0
    hinged = jnp.logical_and(at_top, hinge_ref[0] == 1)
    const_ref[OPEN_NORTH : OPEN_NORTH + 1] = jnp.full((1, COLS), jnp.where(hinged, 0.0, 1.0), jnp.float32)
    inner = (iota((TILE, COLS), 1) < COLS - 1).astype(jnp.float32)
    sub = iota((TILE, COLS), 0)
    for level in range(LEVELS):
        sides = []
        for heat_ref, salt_ref, east_ref, north_ref, wet_ref, mix_ref in (bottom, top):
            heat, salt = heat_ref[level], salt_ref[level]
            east, north = east_ref[level], north_ref[level]
            wet = wet_ref[level].astype(jnp.float32)
            mixed = mix_down(heat, salt)
            here, there = weights(wet * inner * east_of(wet), east + east_of(east))
            flux_e = here * mixed + there * east_of(mixed)
            above = lambda x: pltpu.roll(x, TILE - 1, 0)
            here, there = weights(wet * above(wet), north + above(north))
            flux_n = here * mixed + there * above(mixed)
            part = mixed - (flux_e - west_of(flux_e))
            sides.append((heat, salt, east, north, wet, part, mix_ref[min(level, LEVELS - 2)], flux_n))
        *low, flux_n = sides[0]
        low[5] = low[5] - flux_n
        low = [x[:1] for x in low]
        *high, flux_n = sides[1]
        flux_s = pltpu.roll(flux_n, 1, 0)
        high[5] = high[5] + flux_s - jnp.where(sub == TILE - 1, 0.0, flux_n)
        last = [x[TILE - 1 :] for x in high]
        high = [jnp.where(hinged, x[TILE - 2 : TILE - 1], end) for x, end in zip(high, last)]
        for start, one, other, end in zip((HEAT, SALT, EAST, NORTH, WET, PART, MIX), low, high, last):
            if start == MIX and level == LEVELS - 1:
                continue
            row = slice(start + level, start + level + 1)
            a_ref[row] = jnp.where(even, other, one)
            b_ref[row] = jnp.where(even, one, other)
            own_ref[0, row] = one
            own_ref[1, row] = end
    for ref in (a_ref, b_ref):
        ref[MIX + LEVELS - 1 :] = jnp.zeros((PAYLOAD - MIX - LEVELS + 1, COLS), jnp.float32)

    @pl.when(at_top)
    def _():
        back = LANES - 1 - iota((TILE, LANES), 1)
        for row in range(0, PAYLOAD, TILE):
            place = row + iota((TILE, LANES), 0)
            sign = jnp.where(jnp.logical_and(place >= EAST, place < WET), -1.0, 1.0)
            left = b_ref[row : row + TILE, :LANES]
            right = b_ref[row : row + TILE, LANES:]
            flip = lambda x: sign * jnp.take_along_axis(x, back, axis=1, mode="promise_in_bounds")
            b_ref[row : row + TILE, :LANES] = flip(right)
            b_ref[row : row + TILE, LANES:] = flip(left)

    for copy in copies[early:]:
        copy.wait()


def factor(thick, mix, wet):
    inverse, weight, ratio = [], [], []
    for level in range(LEVELS):
        diagonal = thick[level]
        if level < LEVELS - 1:
            weight.append((0.2 * mix[level]) * (wet[level] * wet[level + 1]))
            diagonal = diagonal + weight[level]
        if level > 0:
            diagonal = diagonal + weight[level - 1] * (1.0 - ratio[level - 1])
        inverse.append(1.0 / diagonal)
        if level < LEVELS - 1:
            ratio.append(weight[level] * inverse[level])
    return inverse, weight, ratio


def solve(thick, inverse, weight, ratio, right):
    x = []
    for level in range(LEVELS):
        now = thick[level] * right[level]
        if level > 0:
            now = now + weight[level - 1] * x[level - 1]
        x.append(now * inverse[level])
    for level in reversed(range(LEVELS - 1)):
        x[level] = x[level] + ratio[level] * x[level + 1]
    return x


def pressures(thick, density):
    above, out = None, []
    for level in range(LEVELS):
        layer = (0.1 * thick[level]) * density[level]
        out.append(0.5 * layer if above is None else above + 0.5 * layer)
        above = layer if above is None else above + layer
    return out


def thicknesses(const_ref, width):
    return [const_ref[level : level + 1, :width] for level in range(LEVELS)]


def inner_steps(
    const_ref, spins, heat_ref, salt_ref, east_ref, north_ref, wet_ref, mix_ref,
    heat_out, salt_out, east_out, north_out, inv_out, weight_out, face_e_out, face_n_out, rim_out, rim_face_out,
    heat_f, salt_f, east_f, north_f, rim, rim_face,
):
    thick = thicknesses(const_ref, COLS)
    inner = (iota((TILE, COLS), 1) < COLS - 1).astype(jnp.float32)
    sub = iota((TILE, COLS), 0)
    lane = iota((TILE, LANES), 1)
    for ref in (heat_f, salt_f, east_f, north_f):
        ref[...] = jnp.zeros(ref.shape, jnp.float32)

    def both_ends(x, east_lane):
        west = jnp.where(lane == 0, x[:, :LANES], 0.0)
        return jnp.where(lane == east_lane, x[:, LANES:], west)

    def step(block, _):
        rows = tile_rows(block)
        above = tile_rows(jnp.minimum(block + 1, BLOCKS - 1))
        shut = jnp.logical_and(sub == TILE - 1, block == BLOCKS - 1)
        spin = spins[rows]
        spin = jnp.concatenate([spin, spin], axis=1)
        ends = jnp.zeros((TILE, LANES), jnp.float32)
        end_faces = ends
        all_wet, all_mix, all_flows, changes = [], [], [], []
        stack = lambda ref: ref[:, rows].reshape(LEVELS * TILE, COLS)
        heat_all, salt_all, north_all = (east_of(stack(ref)) for ref in (heat_ref, salt_ref, north_ref))
        coded_all = jnp.where(stack(wet_ref) > 0, stack(east_ref), DRY)
        coded_east = east_of(coded_all)
        for level in range(LEVELS):
            mine = slice(level * TILE, level * TILE + TILE)
            pick = lambda ref: (ref[level, rows], north_of(ref[level, rows], ref[level, above], sub))
            heat, heat_n = pick(heat_ref)
            salt, salt_n = pick(salt_ref)
            east, east_n = pick(east_ref)
            north, north_n = pick(north_ref)
            wet, wet_n = (x.astype(jnp.float32) for x in pick(wet_ref))
            all_wet.append(wet)
            both = jnp.where(shut, 0.0, wet * wet_n)
            face_n_out[level, rows] = 0.1 * both
            here, there = weights(both, north + north_n)
            spread = GRAIN * both
            flows = [
                here * heat + there * heat_n,
                here * salt + there * salt_n,
                spread * (east_n - east),
                spread * (north_n - north),
            ]
            change = []
            for ref, flow in zip((heat_f, salt_f, east_f, north_f), flows):
                change.append(flow - south_of(flow, ref[level], sub))
                ref[level] = flow
            coded, coded_e = coded_all[mine], coded_east[mine]
            both = jnp.where(coded_e < 0.5 * DRY, wet * inner, 0.0)
            face = 0.1 * both
            face_e_out[level, rows] = face
            place = 4 * level
            end_faces = end_faces + pltpu.roll(both_ends(face, LANES - 2), place + 2, 1)
            here, there = weights(both, coded_e + east)
            spread = GRAIN * both
            flows = [
                here * heat + there * heat_all[mine],
                here * salt + there * salt_all[mine],
                spread * (coded_e - east),
                spread * (north_all[mine] - north),
            ]
            changes.append([n + flow for n, flow in zip(change, flows)])
            all_flows.append(flows)
        all_flows = [west_of(jnp.concatenate(one, axis=0)) for one in zip(*all_flows)]
        for level in range(LEVELS):
            mine = slice(level * TILE, level * TILE + TILE)
            change = [n - flow[mine] for n, flow in zip(changes[level], all_flows)]
            heat, salt = heat_ref[level, rows], salt_ref[level, rows]
            east, north = east_ref[level, rows], north_ref[level, rows]
            wet, coded = all_wet[level], coded_all[mine]
            new_heat = heat - change[0]
            new_salt = salt - change[1]
            heat_out[level, rows] = new_heat
            salt_out[level, rows] = new_salt
            turn = wet * spin
            east_out[level, rows] = east + (turn * north + change[2])
            north_out[level, rows] = north + (change[3] - turn * east)
            fields = [heat, salt, coded, north, mix_down(new_heat, new_salt)]
            if level < LEVELS - 1:
                all_mix.append(mix_ref[level, rows])
                fields.append(all_mix[level])
            for which, x in enumerate(fields):
                place = 2 * (which * LEVELS + level)
                ends = ends + pltpu.roll(both_ends(x, LANES - 1), place + 1, 1)
        rim[rows] = ends
        rim_face[rows] = end_faces
        inverse, weight, _ = factor(thick, all_mix, all_wet)
        for level in range(LEVELS):
            inv_out[level, rows] = inverse[level]
            if level < LEVELS - 1:
                weight_out[level, rows] = weight[level]
        return 0

    lax.fori_loop(0, BLOCKS, step, 0, unroll=2)
    wide = iota((LANES, LANES), 1)
    rim[...] = jnp.where(wide < ROWS, jnp.transpose(rim[...]), 0.0)
    rim_face[...] = jnp.where(wide < ROWS, jnp.transpose(rim_face[...]), 0.0)
    for side, first in ((0, 1), (1, 0)):
        rim_face_out[side, :LEVELS] = rim_face[pl.ds(2 * first, LEVELS, 4)]
        ends = rim[pl.ds(first, ROWS, 2)]
        coded = ends[EAST : EAST + LEVELS]
        rim_out[side, HEAT:EAST] = ends[HEAT:EAST]
        rim_out[side, EAST : EAST + LEVELS] = jnp.where(coded < DRY, coded, 0.0)
        rim_out[side, NORTH : NORTH + LEVELS] = ends[30:40]
        rim_out[side, WET : WET + LEVELS] = jnp.where(coded < DRY, 1.0, 0.0)
        rim_out[side, PART : PART + 2 * LEVELS] = ends[40:60]
        rim_out[side, PART + 2 * LEVELS :] = jnp.zeros((PAYLOAD - PART - 2 * LEVELS, LANES), jnp.float32)


def from_lat(a_ref, b_ref):
    even = lax.axis_index("lat") % 2 == 0
    a, b = a_ref[...], b_ref[...]
    return jnp.where(even, b, a), jnp.where(even, a, b)


def row_faces(const_ref, a_ref, b_ref, own_ref, rim_ref, fix_out, rhs_out, c_out, d_out, ghost):
    open_north = const_ref[OPEN_NORTH : OPEN_NORTH + 1]
    ghost[0], ghost[1] = from_lat(a_ref, b_ref)
    mixed_flux = []
    for side in range(2):
        mine = lambda start: own_ref[side, start : start + LEVELS]
        other = lambda start: ghost[side, start : start + LEVELS]
        low, high = (other, mine) if side == 0 else (mine, other)
        sign = 1.0 if side == 0 else -1.0
        both = low(WET) * high(WET)
        here, there = weights(both, low(NORTH) + high(NORTH))
        spread = -sign * GRAIN * both
        heat_n = here * low(HEAT) + there * high(HEAT)
        salt_n = here * low(SALT) + there * high(SALT)
        changes = (
            sign * heat_n,
            sign * salt_n,
            spread * (high(EAST) - low(EAST)),
            spread * (high(NORTH) - low(NORTH)),
            0.1 * both,
        )
        for which, change in enumerate(changes):
            base = (side * len(changes) + which) * GROUP
            fix_out[base : base + LEVELS] = change
        flux = mix_down(heat_n, salt_n)
        mixed_flux.append(flux)
        change = -flux if side == 0 else open_north * flux
        rhs_out[side * GROUP : side * GROUP + LEVELS] = other(PART) + change
    lane = iota((LEVELS, LANES), 1)
    wide = iota((PAYLOAD, LANES), 1)
    sides = []
    for side, column in ((0, 0), (1, COLS - 1)):
        ends = rim_ref[side]
        for place, which in ((SOUTH_LANE, 0), (NORTH_LANE, 1)):
            ends = jnp.where(wide == place, ghost[which, :, column : column + 1], ends)
        part = rim_ref[side, PART : PART + LEVELS]
        part = part + jnp.where(lane == 0, mixed_flux[0][:, column : column + 1], 0.0)
        part = part - jnp.where(lane == ROWS - 1, mixed_flux[1][:, column : column + 1], 0.0)
        sides.append((ends, part))
    even = lax.axis_index("lon") % 2 == 0
    c_out[...] = jnp.where(even, sides[1][0], sides[0][0])
    d_out[...] = jnp.where(even, sides[0][0], sides[1][0])
    c_out[PART : PART + LEVELS] = jnp.where(even, sides[1][1], sides[0][1])
    d_out[PART : PART + LEVELS] = jnp.where(even, sides[0][1], sides[1][1])


def bands_at(inv_ref, weight_ref, rows):
    inverse = [inv_ref[level, rows] for level in range(LEVELS)]
    weight = [weight_ref[level, rows] for level in range(LEVELS - 1)]
    return inverse, weight, [w * inv for w, inv in zip(weight, inverse)]


def settle(
    const_ref, heat_ref, salt_ref, east_ref, north_ref, inv_ref, weight_ref, face_e_ref, face_n_ref,
    ghost, fix_ref, rhs_ref,
    heat_out, salt_out, east_out, north_out,
    press_x, rim_rhs, rim_mix, rim_wet, rim_press, north_f, outer_p,
):
    for level in range(LEVELS):
        for slot in range(TILE):
            side, half = slot // 2 % 2, slot % 2 * LANES
            row = side * GROUP + level
            rim_rhs[level, slot : slot + 1] = rhs_ref[row : row + 1, half : half + LANES]
            for ref, start in ((rim_mix, MIX), (rim_wet, WET)):
                row = start + level
                ref[level, slot : slot + 1] = ghost[side, row : row + 1, half : half + LANES]
    listed = lambda ref: [ref[level] for level in range(LEVELS)]
    thin = thicknesses(const_ref, LANES)
    rim_density = solve(thin, *(bands := factor(thin, listed(rim_mix), listed(rim_wet))), listed(rim_rhs))
    for level, value in enumerate(pressures(thin, rim_density)):
        rim_press[level] = value
        for slot in range(4):
            half = slot % 2 * LANES
            outer_p[slot // 2, level : level + 1, half : half + LANES] = rim_press[level, slot : slot + 1]

    for level in range(LEVELS):
        for side, row in ((0, 0), (1, ROWS - 1)):
            for which, (src, out) in enumerate(
                ((heat_ref, heat_out), (salt_ref, salt_out), (east_ref, east_out), (north_ref, north_out))
            ):
                place = (side * 5 + which) * GROUP + level
                out[level, row : row + 1] = src[level, row : row + 1] + fix_ref[place : place + 1]
    thick = thicknesses(const_ref, COLS)
    sub = iota((TILE, COLS), 0)

    def tracers(block, _):
        rows = tile_rows(block)
        bands = bands_at(inv_ref, weight_ref, rows)
        first = jnp.logical_and(block == 0, sub == 0)
        last = jnp.logical_and(block == BLOCKS - 1, sub == TILE - 1)
        fixed = jnp.logical_or(first, last)
        take = lambda src, out: [jnp.where(fixed, out[level, rows], src[level, rows]) for level in range(LEVELS)]
        heat = solve(thick, *bands, take(heat_ref, heat_out))
        salt = solve(thick, *bands, take(salt_ref, salt_out))
        density = [mix_down(h, s) for h, s in zip(heat, salt)]
        for level, value in enumerate(pressures(thick, density)):
            heat_out[level, rows] = heat[level]
            salt_out[level, rows] = salt[level]
            press_x[level, rows] = value
        return 0

    lax.fori_loop(0, BLOCKS, tracers, 0, unroll=2)
    for level in range(LEVELS):
        north_f[level] = jnp.zeros((TILE, COLS), jnp.float32)
        for side, row in ((0, 0), (1, ROWS - 1)):
            place = (side * 5 + 4) * GROUP + level
            outer = outer_p[side, level : level + 1]
            slope = fix_ref[place : place + 1] * (press_x[level, row : row + 1] - outer)
            north_out[level, row : row + 1] += slope if side == 1 else -slope

    def flow(block, _):
        rows = tile_rows(block)
        above = tile_rows(jnp.minimum(block + 1, BLOCKS - 1))
        first = jnp.logical_and(block == 0, sub == 0)
        last = jnp.logical_and(block == BLOCKS - 1, sub == TILE - 1)
        fixed = jnp.logical_or(first, last)
        for level in range(LEVELS):
            press = press_x[level, rows]
            press_n = north_of(press, press_x[level, above], sub)
            slope_n = face_n_ref[level, rows] * (press_n - press)
            slope_s = south_of(slope_n, north_f[level], sub)
            north_f[level] = slope_n
            slope_e = face_e_ref[level, rows] * (east_of(press) - press)
            east = jnp.where(fixed, east_out[level, rows], east_ref[level, rows])
            north = jnp.where(fixed, north_out[level, rows], north_ref[level, rows])
            east_out[level, rows] = east - (slope_e + west_of(slope_e))
            north_out[level, rows] = north - (slope_n + slope_s)
        return 0

    lax.fori_loop(0, BLOCKS, flow, 0, unroll=2)


def row_shifts(x, lane):
    after = jnp.where(lane == ROWS, pltpu.roll(x, LANES - 1, 1), x)
    before = jnp.where(lane == LANES - 1, pltpu.roll(x, LANES - 1 - SOUTH_LANE, 1), x)
    return pltpu.roll(after, LANES - 1, 1), pltpu.roll(before, 1, 1)


def finish(
    const_ref, heat_ref, salt_ref, east_ref, north_ref, inv_ref, weight_ref, rim_face_ref,
    d_own_ref, c_own_ref, d_ref, c_ref,
    heat_out, salt_out, east_out, north_out,
    rims, rim_rhs, rim_mix, rim_wet, rim_rows, fixes, heat_x, salt_x, east_x, north_x, sems,
):
    even = lax.axis_index("lon") % 2 == 0
    rims[0] = jnp.where(even, d_own_ref[...], c_own_ref[...])
    rims[1] = jnp.where(even, d_ref[...], c_ref[...])
    rims[2] = jnp.where(even, c_own_ref[...], d_own_ref[...])
    rims[3] = jnp.where(even, c_ref[...], d_ref[...])
    span = lambda which, start: rims[which, start : start + LEVELS]
    slots = lambda slot: slice(GROUP * slot, GROUP * slot + LEVELS)
    lane = iota((LEVELS, LANES), 1)
    sides = ((1, 0), (2, 3))
    for side, (left, right) in enumerate(sides):
        both = span(left, WET) * span(right, WET)
        here, there = weights(both, span(left, EAST) + span(right, EAST))
        heat_e = here * span(left, HEAT) + there * span(right, HEAT)
        salt_e = here * span(left, SALT) + there * span(right, SALT)
        own = 1.0 if side == 0 else -1.0
        rim_rows[slots(2 * side)] = own * heat_e
        rim_rows[slots(2 * side + 1)] = own * salt_e
        rim_rows[slots(4 + side)] = span(2 * side + 1, PART) - own * mix_down(heat_e, salt_e)
        rim_rows[slots(6 + side)] = span(2 * side, PART)
    source = (0, 0, 2, 2, 1, 3, 0, 2)
    for level in range(LEVELS):
        for slot in range(TILE):
            rim_rhs[level, slot : slot + 1] = rim_rows[GROUP * slot + level : GROUP * slot + level + 1]
            for ref, start in ((rim_mix, MIX), (rim_wet, WET)):
                ref[level, slot : slot + 1] = rims[source[slot], start + level : start + level + 1]
    listed = lambda ref: [ref[level] for level in range(LEVELS)]
    thin = thicknesses(const_ref, LANES)
    solved = solve(thin, *factor(thin, listed(rim_mix), listed(rim_wet)), listed(rim_rhs))
    for level, value in enumerate(solved):
        rim_rhs[level] = value
        for slot in range(TILE):
            rim_rows[GROUP * slot + level : GROUP * slot + level + 1] = rim_rhs[level, slot : slot + 1]

    def pressed(density):
        out = pressures(thin, [density[level : level + 1] for level in range(LEVELS)])
        return jnp.concatenate(out, axis=0)

    for side, (left, right) in enumerate(sides):
        heat, salt = rim_rows[slots(2 * side)], rim_rows[slots(2 * side + 1)]
        change = pressed(mix_down(heat, salt))
        mine = pressed(rim_rows[slots(6 + side)]) + change
        other = pressed(rim_rows[slots(4 + side)])
        low, high = (other, mine) if side == 0 else (mine, other)
        both = span(left, WET) * span(right, WET)
        own = -1.0 if side == 0 else 1.0
        slope = 0.1 * both * (high - low)
        inner = rim_face_ref[side, :LEVELS] * change
        inner = inner if side == 0 else -inner
        wet = span(2 * side, WET)
        wet_n, wet_s = row_shifts(wet, lane)
        change_n, change_s = row_shifts(change, lane)
        pull = 0.1 * (wet * wet_n * (change_n - change) + wet * wet_s * (change - change_s))
        east = own * GRAIN * both * (span(right, EAST) - span(left, EAST)) - slope + inner
        north = own * GRAIN * both * (span(right, NORTH) - span(left, NORTH)) - pull
        west_side = 1 - side
        fixes[pl.ds(1 + west_side, LEVELS, 4)] = east
        fixes[pl.ds(3 * west_side, LEVELS, 4)] = inner
        for which, value in enumerate((heat, salt, north)):
            fixes[pl.ds(40 + 20 * which + west_side, LEVELS, 2)] = value
    fixes[...] = jnp.transpose(fixes[...])
    thick = thicknesses(const_ref, COLS)
    lanes = iota((TILE, LANES), 1)

    def fix(corner, place, reach):
        turned = pltpu.roll(corner, LANES - place, 1)
        west = jnp.where(lanes < reach, turned, 0.0)
        east = jnp.where(lanes >= LANES - reach, turned, 0.0)
        return jnp.concatenate([west, east], axis=1)

    def leave(block):
        rows = tile_rows(block)
        pairs = ((heat_x, heat_out), (salt_x, salt_out), (east_x, east_out), (north_x, north_out))
        return [
            pltpu.make_async_copy(src.at[:, rows], dst.at[:, rows], sems.at[block, i])
            for i, (src, dst) in enumerate(pairs)
        ]

    def flow(block, _):
        rows = tile_rows(block)
        corner = fixes[rows]
        new_east, new_north = [], []
        for level in range(LEVELS):
            heat_x[level, rows] = heat_ref[level, rows] + fix(corner, 41 + 2 * level, 1)
            salt_x[level, rows] = salt_ref[level, rows] + fix(corner, 61 + 2 * level, 1)
            new_east.append(east_ref[level, rows] + fix(corner, 4 * level + 2, 2))
            new_north.append(north_ref[level, rows] + fix(corner, 81 + 2 * level, 1))
        bands = bands_at(inv_ref, weight_ref, rows)
        for out, right in ((east_x, new_east), (north_x, new_north)):
            for level, value in enumerate(solve(thick, *bands, right)):
                out[level, rows] = value
        for copy in leave(block):
            copy.start()
        return 0

    lax.fori_loop(0, BLOCKS, flow, 0, unroll=2)
    for block in range(BLOCKS):
        for copy in leave(block):
            copy.wait()


def swap_in_pairs(x, axis, first):
    count = lax.axis_size(axis)
    return lax.ppermute(x, axis, [(i, (((i - first) ^ 1) + first) % count) for i in range(count)])


def swap_with_fold(x, anchor):
    lon, lat = lax.axis_size("lon"), lax.axis_size("lat")
    pairs = []
    for i in range(lon):
        for j in range(1, lat - 1):
            pairs.append((i * lat + j, i * lat + ((j - 1) ^ 1) + 1))
        pairs.append((i * lat + lat - 1, (anchor - 1 - i) % lon * lat + lat - 1))
    return lax.ppermute(x, ("lon", "lat"), pairs)


SMEM = pl.BlockSpec(memory_space=pltpu.SMEM)
VMEM = pl.BlockSpec(memory_space=pltpu.VMEM)
ANYWHERE = pl.BlockSpec(memory_space=pl.ANY)


def small(*shape):
    return pltpu.VMEM(shape, jnp.float32)


def made(*shape):
    return jax.ShapeDtypeStruct(shape, jnp.float32)


PLAIN = (LEVELS, ROWS, COLS)
LESS = (LEVELS - 1, ROWS, COLS)
CARRY = (LEVELS, TILE, COLS)
RIM = (LEVELS, TILE, LANES)


def limit(mib):
    return pltpu.CompilerParams(vmem_limit_bytes=mib * 2**20)


def cost(micros):
    return pl.CostEstimate(flops=0, bytes_accessed=int(micros * 3.5e6), transcendentals=0)


def inner_beside_rows(anchor, a_sent, b_sent, own, const, spins, cells):
    a_got = swap_in_pairs(a_sent, "lat", 0)
    b_got = swap_with_fold(b_sent, anchor)
    *steps, rim, rim_face = pl.pallas_call(
        inner_steps,
        in_specs=[VMEM] * 8,
        out_specs=[VMEM] * 10,
        out_shape=[made(*PLAIN)] * 5 + [made(*LESS)] + [made(*PLAIN)] * 2
        + [made(2, PAYLOAD, LANES), made(2, GROUP, LANES)],
        scratch_shapes=[small(*CARRY)] * 4 + [small(LANES, LANES)] * 2,
        cost_estimate=cost(5),
        compiler_params=limit(16),
        name="inner_steps",
    )(const, spins, *cells)
    faces = pl.pallas_call(
        row_faces,
        in_specs=[VMEM] * 5,
        out_specs=[VMEM] * 5,
        out_shape=[made(10 * GROUP, COLS), made(2 * GROUP, COLS)] + [made(PAYLOAD, LANES)] * 2
        + [made(2, PAYLOAD, COLS)],
        cost_estimate=cost(0.5),
        compiler_params=limit(4),
        name="row_faces",
    )(const, a_got, b_got, own, rim)
    return faces, steps, rim_face


def columns_and_finish(faces, steps, rim_face, const):
    fix, rhs, c_sent, d_sent, ghost = faces
    c_got = swap_in_pairs(c_sent, "lon", 0)
    d_got = swap_in_pairs(d_sent, "lon", 1)
    *steps, inverse, weight, face_e, face_n = steps
    steps = pl.pallas_call(
        settle,
        in_specs=[VMEM] * 12,
        out_specs=[VMEM] * 4,
        out_shape=[made(*PLAIN)] * 4,
        scratch_shapes=[small(*PLAIN)]
        + [small(*RIM)] * 4
        + [small(*CARRY), small(2, GROUP, COLS)],
        cost_estimate=cost(4),
        compiler_params=limit(12),
        name="settle",
    )(const, *steps, inverse, weight, face_e, face_n, ghost, fix, rhs)
    return pl.pallas_call(
        finish,
        in_specs=[VMEM] * 12,
        out_specs=[ANYWHERE] * 4,
        out_shape=[made(*PLAIN)] * 4,
        scratch_shapes=[small(4, PAYLOAD, LANES)]
        + [small(*RIM)] * 3
        + [small(LANES, LANES)] * 2
        + [small(*PLAIN)] * 4
        + [pltpu.SemaphoreType.DMA((BLOCKS, 4))],
        cost_estimate=cost(3),
        compiler_params=limit(12),
        name="finish",
    )(const, *steps, inverse, weight, rim_face, d_sent, c_sent, d_got, c_got)


def on_device(heat, salt, east, north, marine, mixing, spacing, spin, hinge, partner):
    cells = (heat, salt, east, north, marine, mixing)
    edges = [pltpu.VMEM((2, x.shape[0], TILE, COLS), x.dtype) for x in cells]
    anchor, a_sent, b_sent, own, const, spins, *cells = pl.pallas_call(
        pack_rows,
        in_specs=[ANYWHERE] * 10,
        out_specs=[SMEM] + [VMEM] * 11,
        out_shape=[pltpu.SMEM((1,), jnp.int32)]
        + [made(PAYLOAD, COLS)] * 2
        + [made(2, PAYLOAD, COLS), made(OPEN_NORTH + TILE, COLS), made(LANES, LANES)]
        + [jax.ShapeDtypeStruct(x.shape, x.dtype) for x in cells],
        scratch_shapes=[
            pltpu.SMEM((1,), jnp.int32),
            pltpu.SMEM((COLS,), jnp.int32),
            pltpu.SMEM((LEVELS,), jnp.float32),
            small(1, ROWS),
            *edges,
            pltpu.SemaphoreType.DMA((22,)),
        ],
        cost_estimate=cost(2),
        compiler_params=limit(8),
        name="pack_rows",
    )(hinge, *[pltpu.with_memory_space_constraint(x, pltpu.HBM) for x in (partner, spacing, spin.reshape(1, -1), *cells)])
    branches = [functools.partial(inner_beside_rows, k) for k in range(lax.axis_size("lon"))]
    got = lax.switch(anchor[0], branches, a_sent, b_sent, own, const, spins, cells)
    return columns_and_finish(*got, const)


def solution(mesh):
    cells = P(None, "lat", "lon")
    return jax.shard_map(
        on_device,
        mesh=mesh,
        in_specs=(cells,) * 6 + (P(), P("lat"), P(), P("lon")),
        out_specs=(cells,) * 4,
        check_vma=False,
    )
```
